32 devices in a mesh: groups: 2 (over y), row: 4 (over z), col: 4 (over x, core).
Axes of the slice: x: 2, y: 2, z: 4, core: 2. Of those that a mesh axis runs over, the one named last changes fastest.
Arguments:
- pair: bfloat16 [512, 256, 128], P(('groups', 'row'), 'col'), parts along dimension 0, may hold values from -300 to 300
- single: bfloat16 [512, 384], P(('groups', 'row')), parts along dimension 0, may hold values from -6 to 6
- token_mask: int32 [512], P(('groups', 'col')), parts along dimension 0, may hold values from 0 to 1, as said below
- pair_gain: float32 [128], replicated, may hold values from 0.25 to 1.75
- transition_in: bfloat16 [128, 1024], replicated, may hold values from -0.5 to 0.5
- transition_out: bfloat16 [512, 128], replicated, may hold values from -0.25 to 0.25
- bias_weight: float32 [128, 16], replicated, may hold values from -0.9 to 0.9
- bin_weight: float32 [128, 64], replicated, may hold values from -0.5 to 0.5
- single_gain: float32 [384], replicated, may hold values from 0.25 to 1.75
- attention_in: bfloat16 [384, 1536], replicated, may hold values from -0.3125 to 0.3125
- attention_out: bfloat16 [384, 384], replicated, may hold values from -0.8984375 to 0.8984375
Outputs:
- distogram: float32 [512, 256, 64], P(('groups', 'row'), 'col'), parts along dimension 0
- single_update: bfloat16 [512, 384], P(('groups', 'row')), parts along dimension 0
The draws below stay inside these ranges and needn't reach their ends.
There are 2 independent parts, one for each index of `groups`. The reference program is written for one: setup_inputs(seed, part) draws one part's arguments, and reference() takes and returns one part's arrays. A program takes and returns all parts, laid end to end along the dimension named above; an argument that names none is the same for every part. Nothing has to cross between parts.
Inputs may be any that keep to these rules, and one draw needn't show every extreme that they name: `token_mask`: 1 on a prefix of at least 128 tokens, 0 after it; at least the last token is 0.
All inputs are finite; a program needn't handle non-finite values.
Results may differ from the reference program's by a relative error of at most 0.014.
Values may be sent and summed in bfloat16 or wider, within the bound.
No kernel may reach another device: no remote copies, remote signals or barrier semaphores. Data moves between devices by JAX's collectives and lax.ppermute only.
A program may use at most 64 MiB of HBM per device.

```python
import math
import jax
import jax.numpy as jnp
from jax import lax

CP = 128
TRANS_HIDDEN = 512
HEADS = 16
HEAD_DIM = 24
BINS = 64
TILE = 64
CS = 384
TOKENS = 256


def draw_pair(key, part):
    shape = (TOKENS, TOKENS, CP)
    values = jnp.clip(jax.random.normal(key, shape, jnp.float32), -6.0, 6.0)
    return values.astype(jnp.bfloat16)


def draw_token_mask(key, part):
    valid_count = jax.random.randint(key, (), TOKENS // 2, TOKENS)
    return (jnp.arange(TOKENS) < valid_count).astype(jnp.int32)


def steps_of(own_key, shape, pieces, low, largest):
    def one(dim, parts):
        steps = jax.random.uniform(jax.random.fold_in(jax.random.fold_in(own_key, 6), dim), (parts,), jnp.float32, low / len(pieces), largest / len(pieces))
        return jnp.repeat(jnp.exp(steps), shape[dim] // parts).reshape((-1,) + (1,) * (len(shape) - dim - 1))

    loudness = one(*pieces[0])
    for cut in pieces[1:]:
        loudness = loudness * one(*cut)
    return loudness


def normal_values(key, shape, width, most, pieces=(), held_as=jnp.bfloat16):
    result = width * jax.random.normal(key, shape, jnp.float32)
    if pieces:
        result = result * steps_of(key, shape, pieces, -0.22, 0.18)
    return jnp.clip(result, -most, most).astype(held_as)


def setup_inputs(seed: int = 0, part: int = 0) -> dict:
    key_of = jax.random.split(jax.random.key(seed), 12)
    part_splits = jax.random.split(jax.random.fold_in(key_of[11], part), 12)
    return {
        "pair": draw_pair(jax.random.fold_in(jax.random.fold_in(key_of[11], part), 71), part),
        "single": normal_values(part_splits[1], (TOKENS, CS), 1.0, 6.0, ((0, 4),)),
        "token_mask": draw_token_mask(jax.random.fold_in(jax.random.fold_in(key_of[11], part), 71), part),
        "pair_gain": jnp.clip(1.0 + 0.15 * jax.random.normal(key_of[3], (CP,), jnp.float32), 0.25, 1.75),
        "transition_in": normal_values(key_of[4], (CP, 2 * TRANS_HIDDEN), CP ** -0.5, 0.5),
        "transition_out": normal_values(key_of[5], (TRANS_HIDDEN, CP), TRANS_HIDDEN ** -0.5, 0.25),
        "bias_weight": normal_values(key_of[6], (CP, HEADS), 0.15, 0.9, (), jnp.float32),
        "bin_weight": normal_values(key_of[7], (CP, BINS), CP ** -0.5, 0.5, (), jnp.float32),
        "single_gain": jnp.clip(1.0 + 0.15 * jax.random.normal(key_of[8], (CS,), jnp.float32), 0.25, 1.75),
        "attention_in": normal_values(key_of[9], (CS, 4 * CS), CS ** -0.5, 0.3125),
        "attention_out": normal_values(key_of[10], (CS, CS), 0.15, 0.8984375),
    }


def layer_norm(values, gain):
    average = lax.optimization_barrier(jnp.mean(values, axis=-1, keepdims=True))
    centered = values - average
    variance = lax.optimization_barrier(jnp.mean(centered * centered, axis=-1, keepdims=True))
    return centered * lax.rsqrt(variance + 1e-05) * gain

def pair_block(block_rows, pair_gain, transition_in, transition_out, bias_weight, bin_weight):
    count = block_rows.shape[0] * block_rows.shape[1]
    flat = block_rows.reshape(count, block_rows.shape[2]).astype(jnp.float32)
    normed = layer_norm(flat, pair_gain).astype(jnp.bfloat16)
    both = jnp.dot(normed, transition_in, preferred_element_type=jnp.float32)
    gated = (jax.nn.silu(both[:, :TRANS_HIDDEN]) * both[:, TRANS_HIDDEN:]).astype(jnp.bfloat16)
    updated = flat + jnp.dot(gated, transition_out, preferred_element_type=jnp.float32)
    biases = jnp.dot(updated, bias_weight, precision=lax.Precision.HIGHEST)
    halves = jnp.dot(updated, bin_weight, precision=lax.Precision.HIGHEST)
    return (biases.reshape(block_rows.shape[0], block_rows.shape[1], HEADS), halves.reshape(block_rows.shape[0], block_rows.shape[1], BINS))

def reference(pair, single, token_mask, pair_gain, transition_in, transition_out, bias_weight, bin_weight, single_gain, attention_in, attention_out):

    def per_block(block_rows):
        return pair_block(block_rows, pair_gain, transition_in, transition_out, bias_weight, bin_weight)
    blocks = pair.reshape(TOKENS // TILE, TILE, TOKENS, CP)
    biases, halves = lax.map(per_block, blocks)
    biases = biases.reshape(TOKENS, TOKENS, HEADS)
    halves = halves.reshape(TOKENS, TOKENS, BINS)
    distogram = jax.nn.softmax(halves + halves.transpose(1, 0, 2), axis=-1)
    normed = layer_norm(single.astype(jnp.float32), single_gain).astype(jnp.bfloat16)
    projected = jnp.dot(normed, attention_in, preferred_element_type=jnp.float32)
    queries = projected[:, :CS].reshape(TOKENS, HEADS, HEAD_DIM)
    keys_proj = projected[:, CS:2 * CS].reshape(TOKENS, HEADS, HEAD_DIM)
    values_proj = projected[:, 2 * CS:3 * CS].reshape(TOKENS, HEADS, HEAD_DIM)
    gates = projected[:, 3 * CS:]
    scores = jnp.einsum('ihd,jhd->ihj', queries, keys_proj) / math.sqrt(HEAD_DIM) + biases.transpose(0, 2, 1)
    scores = jnp.where(token_mask[None, None, :] > 0, scores, -1000000000.0)
    highest = lax.optimization_barrier(jnp.max(scores, axis=-1, keepdims=True))
    weights = jnp.exp(scores - highest)
    totals = lax.optimization_barrier(jnp.sum(weights, axis=-1))
    summed = jnp.einsum('ihj,jhd->ihd', weights, values_proj)
    attended = (summed / totals[..., None]).reshape(TOKENS, CS)
    gated = (jax.nn.sigmoid(gates) * attended).astype(jnp.bfloat16)
    single_update = jnp.dot(gated, attention_out, preferred_element_type=jnp.float32).astype(jnp.bfloat16)
    return (distogram, single_update)
```

```python
import functools
import math

import jax
import jax.numpy as jnp
from jax import lax
from jax.experimental import pallas as pl
from jax.experimental.pallas import tpu as pltpu
from jax.sharding import PartitionSpec as P

LANES = 128
CODE_TOP = 32767.0
VMEM_LIMIT = 56 * 1024 * 1024


def full_spec(shape):
    return pl.BlockSpec(shape, lambda *_: (0,) * len(shape))


def call(kernel, outs, args, scratch=(), aliases=None, out_specs=None, in_specs=None):
    return pl.pallas_call(
        kernel,
        grid=(1,),
        out_shape=outs,
        in_specs=in_specs or [full_spec(a.shape) for a in args],
        out_specs=out_specs or jax.tree.map(lambda o: full_spec(o.shape), outs),
        scratch_shapes=list(scratch),
        input_output_aliases=aliases or {},
        compiler_params=pltpu.CompilerParams(vmem_limit_bytes=VMEM_LIMIT),
    )(*args)


def normed(values, gain):
    average = jnp.mean(values, axis=-1, keepdims=True)
    centered = values - average
    variance = jnp.mean(centered * centered, axis=-1, keepdims=True)
    return (centered * lax.rsqrt(variance + 1e-05) * gain).astype(jnp.bfloat16)


def dot(a, b):
    return jnp.dot(a, b, preferred_element_type=jnp.float32)


def dot_t(a, b):
    return lax.dot_general(a, b, (((1,), (1,)), ((), ())), preferred_element_type=jnp.float32)


def split(value):
    high = value.astype(jnp.bfloat16)
    return high, (value - high.astype(jnp.float32)).astype(jnp.bfloat16)


def lane_index(shape):
    return lax.broadcasted_iota(jnp.int32, shape, len(shape) - 1)


def pair_kernel(
    step,
    pair_ref,
    gain_ref,
    in_ref,
    out_ref,
    bias_ref,
    bin_ref,
    heads_ref,
    code_ref,
    flat_weight,
    hidden_weight,
):
    rows, cols, _ = pair_ref.shape
    bins, heads = bin_ref.shape[1], bias_ref.shape[1]
    hidden = out_ref.shape[0]
    flat_weight[...] = jnp.zeros_like(flat_weight)
    flat_weight[:, :bins] = bin_ref[...] - bin_ref[:, bins - 1 :]
    flat_weight[:, bins : bins + heads] = bias_ref[...]
    weight = flat_weight[...]
    high = weight.astype(jnp.bfloat16)
    rest = weight - high.astype(jnp.float32)
    middle = rest.astype(jnp.bfloat16)
    low = (rest - middle.astype(jnp.float32)).astype(jnp.bfloat16)
    parts = dot(out_ref[...], jnp.concatenate([high, middle, low], axis=1))
    folded = parts[:, :LANES] + parts[:, LANES : 2 * LANES] + parts[:, 2 * LANES :]
    folded_high, folded_low = split(folded)
    hidden_weight[:hidden, :LANES] = folded_high
    hidden_weight[:hidden, LANES:] = folded_low
    hidden_weight[hidden:, :LANES] = high
    hidden_weight[hidden:, LANES:] = middle
    gain = gain_ref[...]
    for start in range(0, rows, step):
        tokens = pair_ref[start : start + step].reshape(step * cols, -1)
        inner = normed(tokens.astype(jnp.float32), gain)
        both = dot(inner, in_ref[...])
        gate = both[:, :hidden] * 0.5
        gated = (gate * (1.0 + jnp.tanh(gate)) * both[:, hidden:]).astype(jnp.bfloat16)
        twice = dot(jnp.concatenate([gated, tokens], axis=1), hidden_weight[...])
        heads_ref[start * cols : (start + step) * cols, :] = twice[:, :LANES] + twice[:, LANES:]
    half = rows // 2
    lanes = lane_index((half, LANES))
    for col in range(cols):
        first = heads_ref[pl.ds(col, half, stride=cols), :]
        second = heads_ref[pl.ds(half * cols + col, half, stride=cols), :]
        packed = jnp.where(lanes < bins, first, pltpu.roll(second, bins, 1))
        top = jnp.max(jnp.abs(packed), axis=1, keepdims=True)
        power = jnp.ceil(jnp.log2(jnp.maximum(top, 1e-30)))
        code = jnp.where(
            lanes % bins == bins - 1, power, packed * (jnp.exp2(-power) * CODE_TOP)
        )
        code_ref[col] = jnp.round(code).astype(jnp.int32).astype(jnp.int16)


def softmax_kernel(step, first_ref, second_ref, code_ref, *refs):
    out_ref = refs[-1]
    rows, cols, bins = out_ref.shape
    half = cols // 2
    lanes = lane_index((step * half, LANES))
    for start in range(0, rows, step):
        code = code_ref[start : start + step].reshape(step * half, LANES)
        code = code.astype(jnp.int32).astype(jnp.float32)
        power = jnp.sum(jnp.where(lanes == bins - 1, code, 0.0), axis=1, keepdims=True)
        other = jnp.where(lanes % bins == bins - 1, 0.0, code * (jnp.exp2(power) * (1.0 / CODE_TOP)))
        for part, own_ref in enumerate((first_ref, second_ref)):
            mirrored = other if part == 0 else pltpu.roll(other, bins, 1)
            logits = own_ref[start * half : (start + step) * half, :] + mirrored
            logits = jnp.where(lanes < bins, logits, -jnp.inf)
            top = jnp.max(logits, axis=1, keepdims=True)
            raised = jnp.exp(logits - top)
            share = raised / jnp.sum(raised, axis=1, keepdims=True)
            out_ref[start : start + step, part * half : (part + 1) * half, :] = share[
                :, :bins
            ].reshape(step, half, bins)


def attention_kernel(
    bins,
    single_ref,
    keys_ref,
    mask_ref,
    gain_ref,
    in_ref,
    first_ref,
    second_ref,
    part_ref,
    gates_ref,
    scores,
):
    rows, width = single_ref.shape
    cols = keys_ref.shape[0]
    heads = scores.shape[1]
    head_width = width // heads
    half = cols // 2
    gain = gain_ref[...]
    query_inner = normed(single_ref[...].astype(jnp.float32), gain)
    key_inner = normed(keys_ref[...].astype(jnp.float32), gain)
    queries = dot(query_inner, in_ref[:, :width]) * (1.0 / math.sqrt(head_width))
    gates_ref[...] = jax.nn.sigmoid(dot(query_inner, in_ref[:, 3 * width :]))
    keys_proj = dot(key_inner, in_ref[:, width : 2 * width]).astype(jnp.bfloat16)
    values_proj = dot(key_inner, in_ref[:, 2 * width : 3 * width]).astype(jnp.bfloat16)
    shape = (heads, width)
    lane = lane_index(shape)
    head = lax.broadcasted_iota(jnp.int32, shape, 0)
    own_head = jnp.where((lane >= head * head_width) & (lane < (head + 1) * head_width), 1.0, 0.0)
    spread = (queries[:, None, :] * own_head[None]).astype(jnp.bfloat16)
    scores[...] = dot_t(spread.reshape(rows * heads, width), keys_proj).reshape(rows, heads, cols)
    shape = (heads, 2 * LANES)
    lane = lane_index(shape) % LANES
    pick = (lane == lax.broadcasted_iota(jnp.int32, shape, 0) + bins).astype(jnp.bfloat16)
    for row in range(rows):
        block = jnp.concatenate(
            [ref[row * half : (row + 1) * half, :] for ref in (first_ref, second_ref)], axis=0
        )
        scores[row] += dot_t(pick, jnp.concatenate(split(block), axis=1))
    kept = jnp.where(mask_ref[...] > 0, scores[...].reshape(rows * heads, cols), -1000000000.0)
    top = jnp.max(kept, axis=-1, keepdims=True)
    weights = jnp.exp(kept - top)
    total = jnp.sum(weights, axis=-1, keepdims=True)
    summed = dot((weights * (1.0 / total)).astype(jnp.bfloat16), values_proj)
    summed = jnp.sum(summed.reshape(rows, heads, width) * own_head[None], axis=1)
    part_ref[:, :width] = summed.astype(jnp.bfloat16)
    level = top + jnp.log(total)
    high = level.astype(jnp.bfloat16).astype(jnp.float32)
    middle = (level - high).astype(jnp.bfloat16).astype(jnp.float32)
    low = level - high - middle
    shape = (heads, LANES)
    lane = lane_index(shape)
    head = lax.broadcasted_iota(jnp.int32, shape, 0)
    spread = jnp.zeros((rows, heads, LANES), jnp.float32)
    for place, piece in enumerate((high, middle, low)):
        at = (lane == head + place * heads).astype(jnp.float32)
        spread += piece.reshape(rows, heads, 1) * at[None]
    part_ref[:, width:] = jnp.sum(spread, axis=1).astype(jnp.bfloat16)


def joined_kernel(heads, parts_ref, gates_ref, out_weight_ref, out_ref):
    count, rows, _ = parts_ref.shape
    width = gates_ref.shape[1]
    head_width = width // heads
    shape = (LANES, width)
    lane = lane_index(shape)
    row = lax.broadcasted_iota(jnp.int32, shape, 0)
    head = row % heads
    spread = (
        (lane >= head * head_width) & (lane < (head + 1) * head_width) & (row < 3 * heads)
    ).astype(jnp.bfloat16)
    levels = [dot(parts_ref[k, :, width:], spread) for k in range(count)]
    top = functools.reduce(jnp.maximum, levels)
    total, summed = 0.0, 0.0
    for k in range(count):
        factor = jnp.exp(levels[k] - top)
        total += factor
        summed += factor * parts_ref[k, :, :width].astype(jnp.float32)
    gated = (gates_ref[...] * (summed / total)).astype(jnp.bfloat16)
    out_ref[...] = dot(gated, out_weight_ref[...]).astype(jnp.bfloat16)


def body(
    row_count,
    col_count,
    pair,
    single,
    token_mask,
    pair_gain,
    transition_in,
    transition_out,
    bias_weight,
    bin_weight,
    single_gain,
    attention_in,
    attention_out,
):
    rows, cols, channels = pair.shape
    width = single.shape[1]
    heads, bins = bias_weight.shape[1], bin_weight.shape[1]
    hidden = transition_out.shape[0]
    half = cols // 2
    mirror = [
        (r * col_count + c, c * col_count + r) for r in range(row_count) for c in range(col_count)
    ]

    def mirrored(value):
        return lax.ppermute(value, ("row", "col"), mirror)

    keys = mirrored(single)
    shared = (
        pair_gain.reshape(1, -1),
        transition_in,
        transition_out,
        bias_weight,
        bin_weight,
    )
    own, received = [], []
    for part in range(2):
        spec = pl.BlockSpec((rows, half, channels), lambda _, part=part: (0, part, 0))
        logits, code = call(
            functools.partial(pair_kernel, 8),
            (
                jax.ShapeDtypeStruct((rows * half, LANES), jnp.float32),
                jax.ShapeDtypeStruct((half, rows // 2, LANES), jnp.int16),
            ),
            (pair, *shared),
            scratch=(
                pltpu.VMEM((channels, LANES), jnp.float32),
                pltpu.VMEM((hidden + channels, 2 * LANES), jnp.bfloat16),
            ),
            in_specs=[spec] + [full_spec(a.shape) for a in shared],
        )
        own.append(logits)
        received.append(mirrored(code))

    part_sums, gates = call(
        functools.partial(attention_kernel, bins),
        (
            jax.ShapeDtypeStruct((rows, width + LANES), jnp.bfloat16),
            jax.ShapeDtypeStruct((rows, width), jnp.float32),
        ),
        (
            single,
            keys,
            token_mask.reshape(1, -1),
            single_gain.reshape(1, -1),
            attention_in,
            *own,
        ),
        scratch=(pltpu.VMEM((rows, heads, cols), jnp.float32),),
    )
    gathered = lax.all_gather(part_sums, "col")
    single_update = call(
        functools.partial(joined_kernel, heads),
        jax.ShapeDtypeStruct((rows, width), jnp.bfloat16),
        (gathered, gates, attention_out),
    )
    distogram = None
    out = jax.ShapeDtypeStruct((rows, cols, bins), jnp.float32)
    count = rows // 2
    for part in range(2):
        own_spec = pl.BlockSpec((count * half, LANES), lambda _, part=part: (part, 0))
        args, specs = [*own, received[part]], [own_spec, own_spec, full_spec(received[part].shape)]
        if part:
            args.append(distogram)
            specs.append(pl.BlockSpec(memory_space=pl.ANY))
        distogram = call(
            functools.partial(softmax_kernel, 4),
            out,
            args,
            in_specs=specs,
            out_specs=pl.BlockSpec((count, cols, bins), lambda _, part=part: (part, 0, 0)),
            aliases={3: 0} if part else {},
        )
    return (distogram, single_update)


def solution(mesh):
    in_specs = (
        P(("groups", "row"), "col", None),
        P(("groups", "row"), None),
        P(("groups", "col")),
        P(),
        P(),
        P(),
        P(),
        P(),
        P(),
        P(),
        P(),
    )
    out_specs = (P(("groups", "row"), "col", None), P(("groups", "row"), None))
    own = functools.partial(body, mesh.shape["row"], mesh.shape["col"])
    return jax.shard_map(own, mesh=mesh, in_specs=in_specs, out_specs=out_specs, check_vma=False)
```

```python
import functools
import math

import jax
import jax.numpy as jnp
from jax import lax
from jax.experimental import pallas as pl
from jax.experimental.pallas import tpu as pltpu
from jax.sharding import PartitionSpec as P

LANES = 128
CODE_TOP = 32767.0
PAIR_STEP = 8
CODE_GROUP = 8
SOFT_STEP = 8
VMEM_LIMIT = 56 * 1024 * 1024


def near(shape, dtype):
    return pltpu.VMEM(shape, dtype)


def call(kernel, outs, args, scratch=(), far=(), aliases=None):
    def out_spec(out):
        inside = isinstance(out, type(near((8, LANES), jnp.float32)))
        return pl.BlockSpec(memory_space=pltpu.VMEM if inside else pl.ANY)

    return pl.pallas_call(
        kernel,
        out_shape=outs,
        in_specs=[
            pl.BlockSpec(memory_space=pl.ANY if k in far else pltpu.VMEM) for k in range(len(args))
        ],
        out_specs=jax.tree.map(out_spec, outs),
        scratch_shapes=list(scratch),
        input_output_aliases=aliases or {},
        compiler_params=pltpu.CompilerParams(vmem_limit_bytes=VMEM_LIMIT),
    )(
        *[
            a if k in far else pltpu.with_memory_space_constraint(a, pltpu.VMEM)
            for k, a in enumerate(args)
        ]
    )


def centered(values):
    rest = values - jnp.mean(values, axis=-1, keepdims=True)
    variance = jnp.mean(rest * rest, axis=-1, keepdims=True)
    return rest * lax.rsqrt(variance + 1e-05)


def dot(a, b):
    return jnp.dot(a, b, preferred_element_type=jnp.float32)


def dot_t(a, b):
    return lax.dot_general(a, b, (((1,), (1,)), ((), ())), preferred_element_type=jnp.float32)


def split(value):
    high = value.astype(jnp.bfloat16)
    return high, (value - high.astype(jnp.float32)).astype(jnp.bfloat16)


def lane_index(shape):
    return lax.broadcasted_iota(jnp.int32, shape, len(shape) - 1)


def fill_weights(out_ref, bias_ref, bin_ref, flat_weight, weight_ref):
    bins, heads = bin_ref.shape[0], bias_ref.shape[0]
    hidden = out_ref.shape[0]
    flat_weight[...] = jnp.zeros_like(flat_weight)
    flat_weight[:bins, :] = bin_ref[...] - bin_ref[bins - 1 :, :]
    flat_weight[bins : bins + heads, :] = bias_ref[...]
    weight = flat_weight[...].T
    high = weight.astype(jnp.bfloat16)
    rest = weight - high.astype(jnp.float32)
    middle = rest.astype(jnp.bfloat16)
    low = (rest - middle.astype(jnp.float32)).astype(jnp.bfloat16)
    parts = dot(out_ref[...], jnp.concatenate([high, middle, low], axis=1))
    folded = parts[:, :LANES] + parts[:, LANES : 2 * LANES] + parts[:, 2 * LANES :]
    folded_high, folded_low = split(folded)
    weight_ref[:hidden, :LANES] = folded_high
    weight_ref[:hidden, LANES:] = folded_low
    weight_ref[hidden:, :LANES] = high
    weight_ref[hidden:, LANES:] = middle


def pair_heads(pair_ref, gain, in_ref, weight_ref, heads_ref):
    rows, cols, channels = pair_ref.shape
    hidden = in_ref.shape[1] // 2
    for start in range(0, rows, PAIR_STEP):
        tokens = pair_ref[start : start + PAIR_STEP].reshape(PAIR_STEP * cols, channels)
        inner = centered(tokens.astype(jnp.float32)) * gain
        both = dot(inner.astype(jnp.bfloat16), in_ref[...])
        gate = both[:, :hidden] * 0.5
        gated = (gate * (1.0 + jnp.tanh(gate)) * both[:, hidden:]).astype(jnp.bfloat16)
        twice = dot(gated, weight_ref[:hidden, :]) + dot(tokens, weight_ref[hidden:, :])
        at = slice(start * cols, (start + PAIR_STEP) * cols)
        heads_ref[at, :] = twice[:, :LANES] + twice[:, LANES:]


def fill_code(bins, rows, cols, heads_ref, code_ref):
    half = rows // 2
    lanes = lane_index((half * CODE_GROUP, LANES))
    for start in range(0, cols, CODE_GROUP):
        first, second = (
            jnp.concatenate(
                [
                    heads_ref[pl.ds(top * cols + col, half, stride=cols), :]
                    for col in range(start, start + CODE_GROUP)
                ],
                axis=0,
            )
            for top in (0, half)
        )
        packed = jnp.where(lanes < bins, first, pltpu.roll(second, bins, 1))
        top = jnp.max(jnp.abs(packed), axis=1, keepdims=True)
        power = jnp.ceil(jnp.log2(jnp.maximum(top, 1e-30)))
        code = jnp.where(
            lanes % bins == bins - 1, power, packed * (jnp.exp2(-power) * CODE_TOP)
        )
        code = jnp.round(code).astype(jnp.int32).astype(jnp.int16)
        code_ref[start : start + CODE_GROUP] = code.reshape(CODE_GROUP, half, LANES)


def first_kernel(
    pair_ref,
    gain_ref,
    in_ref,
    out_ref,
    bias_ref,
    bin_ref,
    heads_ref,
    code_ref,
    later_ref,
    gain_near,
    in_near,
    weight_ref,
    tile,
    out_near,
    bias_near,
    bin_near,
    flat_weight,
    sems,
):
    rows, cols, _ = tile.shape

    def bring(source, target, sem):
        copy = pltpu.make_async_copy(source, target, sem)
        copy.start()
        return copy

    small = [
        bring(source, target, sems.at[k])
        for k, (source, target) in enumerate(
            ((bias_ref, bias_near), (bin_ref, bin_near), (out_ref, out_near))
        )
    ]
    gain_copy = bring(gain_ref, gain_near, sems.at[3])
    tile_copy = bring(pair_ref.at[:, pl.ds(0, cols)], tile, sems.at[4])
    in_copy = bring(in_ref, in_near, sems.at[5])
    later = bring(pair_ref.at[:, pl.ds(cols, cols)], later_ref, sems.at[6])
    for copy in small:
        copy.wait()
    fill_weights(out_near, bias_near, bin_near, flat_weight, weight_ref)
    gain_copy.wait()
    in_copy.wait()
    tile_copy.wait()
    gain = gain_near[...].reshape(1, -1)
    pair_heads(tile, gain, in_near, weight_ref, heads_ref)
    fill_code(bin_ref.shape[0], rows, cols, heads_ref, code_ref)
    later.wait()


def second_kernel(bins, pair_ref, gain_ref, in_ref, weight_ref, heads_ref, code_ref):
    rows, cols, _ = pair_ref.shape
    gain = gain_ref[...].reshape(1, -1)
    pair_heads(pair_ref, gain, in_ref, weight_ref, heads_ref)
    fill_code(bins, rows, cols, heads_ref, code_ref)


def softmax_kernel(part, step, first_ref, second_ref, code_ref, *refs):
    out_ref, held, sems = refs[-3:]
    rows, cols, bins = held.shape
    half = cols // 2
    lanes = lane_index((step * half, LANES))
    low = lanes < bins
    copies = []
    for start in range(0, rows, step):
        code = code_ref[start : start + step].reshape(step * half, LANES)
        code = code.astype(jnp.int32).astype(jnp.float32)
        power = jnp.sum(jnp.where(lanes == bins - 1, code, 0.0), axis=1, keepdims=True)
        other = code * (jnp.exp2(power) * (1.0 / CODE_TOP))
        other = jnp.where(lanes % bins == bins - 1, 0.0, other)
        at = pl.ds((part * rows + start) * half, step * half)
        for side, own_ref in enumerate((first_ref, second_ref)):
            mirrored = other if side == 0 else pltpu.roll(other, bins, 1)
            logits = jnp.where(low, own_ref[at, :] + mirrored, -jnp.inf)
            top = jnp.max(logits, axis=1, keepdims=True)
            raised = jnp.exp(logits - top)
            share = raised * (1.0 / jnp.sum(raised, axis=1, keepdims=True))
            held[start : start + step, side * half : (side + 1) * half, :] = share[
                :, :bins
            ].reshape(step, half, bins)
        copies.append(
            pltpu.make_async_copy(
                held.at[pl.ds(start, step)],
                out_ref.at[pl.ds(part * rows + start, step)],
                sems.at[start // step],
            )
        )
        copies[-1].start()
    for copy in copies:
        copy.wait()


def attention_kernel(
    bins,
    single_ref,
    keys_ref,
    mask_ref,
    gain_ref,
    in_ref,
    first_ref,
    second_ref,
    part_ref,
    gates_ref,
    scores,
):
    rows, width = single_ref.shape
    heads, cols = scores.shape[1:]
    head_width = width // heads
    half = cols // 2
    gain = gain_ref[...].reshape(1, -1)
    query_inner = (centered(single_ref[...].astype(jnp.float32)) * gain).astype(jnp.bfloat16)
    key_inner = (centered(keys_ref[...].astype(jnp.float32)) * gain).astype(jnp.bfloat16)
    queries = dot(query_inner, in_ref[:, :width]) * (1.0 / math.sqrt(head_width))
    gates_ref[...] = jax.nn.sigmoid(dot(query_inner, in_ref[:, 3 * width :]))
    keys_proj = dot(key_inner, in_ref[:, width : 2 * width]).astype(jnp.bfloat16)
    values_proj = dot(key_inner, in_ref[:, 2 * width : 3 * width]).astype(jnp.bfloat16)
    shape = (heads, width)
    lane = lane_index(shape)
    head = lax.broadcasted_iota(jnp.int32, shape, 0)
    own_head = jnp.where((lane >= head * head_width) & (lane < (head + 1) * head_width), 1.0, 0.0)
    spread = (queries[:, None, :] * own_head[None]).astype(jnp.bfloat16)
    scores[...] = dot_t(spread.reshape(rows * heads, width), keys_proj).reshape(rows, heads, cols)
    shape = (heads, 2 * LANES)
    lane = lane_index(shape) % LANES
    pick = (lane == lax.broadcasted_iota(jnp.int32, shape, 0) + bins).astype(jnp.bfloat16)
    for row in range(rows):
        block = jnp.concatenate(
            [ref[row * half : (row + 1) * half, :] for ref in (first_ref, second_ref)], axis=0
        )
        scores[row] += dot_t(pick, jnp.concatenate(split(block), axis=1))
    kept = jnp.where(mask_ref[...].reshape(1, -1) > 0, scores[...].reshape(rows * heads, cols), -1000000000.0)
    top = jnp.max(kept, axis=-1, keepdims=True)
    weights = jnp.exp(kept - top)
    total = jnp.sum(weights, axis=-1, keepdims=True)
    summed = dot((weights * (1.0 / total)).astype(jnp.bfloat16), values_proj)
    summed = jnp.sum(summed.reshape(rows, heads, width) * own_head[None], axis=1)
    part_ref[:, :width] = summed.astype(jnp.bfloat16)
    level = top + jnp.log(total)
    high = level.astype(jnp.bfloat16).astype(jnp.float32)
    middle = (level - high).astype(jnp.bfloat16).astype(jnp.float32)
    low = level - high - middle
    shape = (heads, LANES)
    lane = lane_index(shape)
    head = lax.broadcasted_iota(jnp.int32, shape, 0)
    spread = jnp.zeros((rows, heads, LANES), jnp.float32)
    for place, piece in enumerate((high, middle, low)):
        at = (lane == head + place * heads).astype(jnp.float32)
        spread += piece.reshape(rows, heads, 1) * at[None]
    part_ref[:, width:] = jnp.sum(spread, axis=1).astype(jnp.bfloat16)


def joined_kernel(heads, count, *refs):
    parts, (gates_ref, out_weight_ref, out_ref, held, sem) = refs[:count], refs[count:]
    width = gates_ref.shape[1]
    head_width = width // heads
    shape = (LANES, width)
    lane = lane_index(shape)
    row = lax.broadcasted_iota(jnp.int32, shape, 0)
    head = row % heads
    spread = (
        (lane >= head * head_width) & (lane < (head + 1) * head_width) & (row < 3 * heads)
    ).astype(jnp.bfloat16)
    levels = [dot(part[:, width:], spread) for part in parts]
    top = functools.reduce(jnp.maximum, levels)
    total, summed = 0.0, 0.0
    for level, part in zip(levels, parts):
        factor = jnp.exp(level - top)
        total += factor
        summed += factor * part[:, :width].astype(jnp.float32)
    gated = (gates_ref[...] * (summed / total)).astype(jnp.bfloat16)
    held[...] = dot(gated, out_weight_ref[...]).astype(jnp.bfloat16)
    copy = pltpu.make_async_copy(held, out_ref, sem)
    copy.start()
    copy.wait()


def body(
    row_count,
    col_count,
    pair,
    single,
    token_mask,
    pair_gain,
    transition_in,
    transition_out,
    bias_weight,
    bin_weight,
    single_gain,
    attention_in,
    attention_out,
):
    rows, cols, channels = pair.shape
    width = single.shape[1]
    heads, bins = bias_weight.shape[1], bin_weight.shape[1]
    hidden = transition_out.shape[0]
    half = cols // 2
    mirror = [
        (r * col_count + c, c * col_count + r) for r in range(row_count) for c in range(col_count)
    ]

    def mirrored(value):
        return lax.ppermute(value, ("row", "col"), mirror)

    bf16, f32, i16 = jnp.bfloat16, jnp.float32, jnp.int16
    heads_out = near((rows * half, LANES), f32)
    first, code, later, *kept = call(
        first_kernel,
        (
            heads_out,
            near((half, rows // 2, LANES), i16),
            near((rows, half, channels), bf16),
            near(pair_gain.shape, f32),
            near(transition_in.shape, bf16),
            near((hidden + channels, 2 * LANES), bf16),
        ),
        (pair, pair_gain, transition_in, transition_out, bias_weight.T, bin_weight.T),
        scratch=(
            pltpu.VMEM((rows, half, channels), bf16),
            pltpu.VMEM(transition_out.shape, bf16),
            pltpu.VMEM((heads, channels), f32),
            pltpu.VMEM((bins, channels), f32),
            pltpu.VMEM((LANES, channels), f32),
            pltpu.SemaphoreType.DMA((7,)),
        ),
        far=range(6),
    )
    received = [mirrored(code)]
    behind, _ = lax.optimization_barrier((single, code))
    keys = mirrored(behind)
    second, code = call(
        functools.partial(second_kernel, bins),
        (heads_out, near((half, rows // 2, LANES), i16)),
        (later, *kept),
    )
    own = (first, second)
    code, keys = lax.optimization_barrier((code, keys))
    received.append(mirrored(code))
    part_sums, gates = call(
        functools.partial(attention_kernel, bins),
        (
            near((rows, width + LANES), jnp.bfloat16),
            near((rows, width), jnp.float32),
        ),
        (single, keys, token_mask, single_gain, attention_in, *own),
        scratch=(pltpu.VMEM((rows, heads, cols), jnp.float32),),
    )
    parts = [part_sums]
    for away in range(1, col_count):
        ring = [(c, (c + away) % col_count) for c in range(col_count)]
        parts.append(lax.ppermute(part_sums, "col", ring))
    single_update = call(
        functools.partial(joined_kernel, heads, col_count),
        jax.ShapeDtypeStruct((rows, width), bf16),
        (*parts, gates, attention_out),
        scratch=(pltpu.VMEM((rows, width), bf16), pltpu.SemaphoreType.DMA),
    )
    distogram = None
    count = rows // 2
    for part in range(2):
        distogram = call(
            functools.partial(softmax_kernel, part, SOFT_STEP),
            jax.ShapeDtypeStruct((rows, cols, bins), jnp.float32),
            (*own, received[part]) + ((distogram,) if part else ()),
            scratch=(
                pltpu.VMEM((count, cols, bins), jnp.float32),
                pltpu.SemaphoreType.DMA((count // SOFT_STEP,)),
            ),
            far=(3,) if part else (),
            aliases={3: 0} if part else {},
        )
    return (distogram, single_update)


def solution(mesh):
    in_specs = (
        P(("groups", "row"), "col", None),
        P(("groups", "row"), None),
        P(("groups", "col")),
        P(),
        P(),
        P(),
        P(),
        P(),
        P(),
        P(),
        P(),
    )
    out_specs = (P(("groups", "row"), "col", None), P(("groups", "row"), None))
    own = functools.partial(body, mesh.shape["row"], mesh.shape["col"])
    return jax.shard_map(own, mesh=mesh, in_specs=in_specs, out_specs=out_specs, check_vma=False)
```

```python
import functools
import math

import jax
import jax.numpy as jnp
from jax import lax
from jax.experimental import pallas as pl
from jax.experimental.pallas import tpu as pltpu
from jax.sharding import PartitionSpec as P

LANES = 128
CODE_TOP = 32767.0
PAIR_STEP = 8
CODE_GROUP = 8
SOFT_STEP = 16
VMEM_LIMIT = 56 * 1024 * 1024


def near(shape, dtype):
    return pltpu.VMEM(shape, dtype)


def call(kernel, outs, args, scratch=(), far=(), aliases=None):
    def out_spec(out):
        inside = isinstance(out, type(near((8, LANES), jnp.float32)))
        return pl.BlockSpec(memory_space=pltpu.VMEM if inside else pl.ANY)

    return pl.pallas_call(
        kernel,
        out_shape=outs,
        in_specs=[
            pl.BlockSpec(memory_space=pl.ANY if k in far else pltpu.VMEM) for k in range(len(args))
        ],
        out_specs=jax.tree.map(out_spec, outs),
        scratch_shapes=list(scratch),
        input_output_aliases=aliases or {},
        compiler_params=pltpu.CompilerParams(vmem_limit_bytes=VMEM_LIMIT),
    )(
        *[
            a if k in far else pltpu.with_memory_space_constraint(a, pltpu.VMEM)
            for k, a in enumerate(args)
        ]
    )


def centered(values):
    rest = values - jnp.mean(values, axis=-1, keepdims=True)
    variance = jnp.mean(rest * rest, axis=-1, keepdims=True)
    return rest * lax.rsqrt(variance + 1e-05)


def dot(a, b):
    return jnp.dot(a, b, preferred_element_type=jnp.float32)


def dot_t(a, b):
    return lax.dot_general(a, b, (((1,), (1,)), ((), ())), preferred_element_type=jnp.float32)


def split(value):
    high = value.astype(jnp.bfloat16)
    return high, (value - high.astype(jnp.float32)).astype(jnp.bfloat16)


def lane_index(shape):
    return lax.broadcasted_iota(jnp.int32, shape, len(shape) - 1)


def fill_weights(out_ref, bias_ref, bin_ref, flat_weight, weight_ref):
    bins, heads = bin_ref.shape[0], bias_ref.shape[0]
    hidden = out_ref.shape[0]
    flat_weight[...] = jnp.zeros_like(flat_weight)
    flat_weight[:bins, :] = bin_ref[...] - bin_ref[bins - 1 :, :]
    flat_weight[bins : bins + heads, :] = bias_ref[...]
    weight = flat_weight[...].T
    high = weight.astype(jnp.bfloat16)
    rest = weight - high.astype(jnp.float32)
    middle = rest.astype(jnp.bfloat16)
    low = (rest - middle.astype(jnp.float32)).astype(jnp.bfloat16)
    parts = dot(out_ref[...], jnp.concatenate([high, middle, low], axis=1))
    folded = parts[:, :LANES] + parts[:, LANES : 2 * LANES] + parts[:, 2 * LANES :]
    folded_high, folded_low = split(folded)
    weight_ref[:hidden, :LANES] = folded_high
    weight_ref[:hidden, LANES:] = folded_low
    weight_ref[hidden:, :LANES] = high
    weight_ref[hidden:, LANES:] = middle


def pair_heads(pair_ref, gain, in_ref, weight_ref, heads_ref):
    rows, cols, channels = pair_ref.shape
    hidden = in_ref.shape[1] // 2
    for start in range(0, rows, PAIR_STEP):
        tokens = pair_ref[start : start + PAIR_STEP].reshape(PAIR_STEP * cols, channels)
        inner = centered(tokens.astype(jnp.float32)) * gain
        both = dot(inner.astype(jnp.bfloat16), in_ref[...])
        gate = both[:, :hidden] * 0.5
        gated = (gate * (1.0 + jnp.tanh(gate)) * both[:, hidden:]).astype(jnp.bfloat16)
        twice = dot(gated, weight_ref[:hidden, :]) + dot(tokens, weight_ref[hidden:, :])
        at = slice(start * cols, (start + PAIR_STEP) * cols)
        heads_ref[at, :] = twice[:, :LANES] + twice[:, LANES:]


def fill_code(bins, rows, cols, heads_ref, code_ref):
    half = rows // 2
    lanes = lane_index((half * CODE_GROUP, LANES))
    for start in range(0, cols, CODE_GROUP):
        first, second = (
            jnp.concatenate(
                [
                    heads_ref[pl.ds(top * cols + col, half, stride=cols), :]
                    for col in range(start, start + CODE_GROUP)
                ],
                axis=0,
            )
            for top in (0, half)
        )
        packed = jnp.where(lanes < bins, first, pltpu.roll(second, bins, 1))
        top = jnp.max(jnp.abs(packed), axis=1, keepdims=True)
        power = jnp.ceil(jnp.log2(jnp.maximum(top, 1e-30)))
        code = jnp.where(
            lanes % bins == bins - 1, power, packed * (jnp.exp2(-power) * CODE_TOP)
        )
        code = jnp.round(code).astype(jnp.int32).astype(jnp.int16)
        code_ref[start : start + CODE_GROUP] = code.reshape(CODE_GROUP, half, LANES)


def first_kernel(
    pair_ref,
    gain_ref,
    in_ref,
    out_ref,
    bias_ref,
    bin_ref,
    heads_ref,
    code_ref,
    later_ref,
    gain_near,
    in_near,
    weight_ref,
    tile,
    out_near,
    bias_near,
    bin_near,
    flat_weight,
    sems,
):
    rows, cols, _ = tile.shape

    def bring(source, target, sem):
        copy = pltpu.make_async_copy(source, target, sem)
        copy.start()
        return copy

    small = [
        bring(source, target, sems.at[k])
        for k, (source, target) in enumerate(
            ((bias_ref, bias_near), (bin_ref, bin_near), (out_ref, out_near))
        )
    ]
    gain_copy = bring(gain_ref, gain_near, sems.at[3])
    tile_copy = bring(pair_ref.at[:, pl.ds(0, cols)], tile, sems.at[4])
    in_copy = bring(in_ref, in_near, sems.at[5])
    later = bring(pair_ref.at[:, pl.ds(cols, cols)], later_ref, sems.at[6])
    for copy in small:
        copy.wait()
    fill_weights(out_near, bias_near, bin_near, flat_weight, weight_ref)
    gain_copy.wait()
    in_copy.wait()
    tile_copy.wait()
    gain = gain_near[...].reshape(1, -1)
    pair_heads(tile, gain, in_near, weight_ref, heads_ref)
    fill_code(bin_ref.shape[0], rows, cols, heads_ref, code_ref)
    later.wait()


def second_kernel(bins, pair_ref, gain_ref, in_ref, weight_ref, heads_ref, code_ref):
    rows, cols, _ = pair_ref.shape
    gain = gain_ref[...].reshape(1, -1)
    pair_heads(pair_ref, gain, in_ref, weight_ref, heads_ref)
    fill_code(bins, rows, cols, heads_ref, code_ref)


def softmax_kernel(part, step, first_ref, second_ref, code_ref, *refs):
    out_ref, held, sems = refs[-3:]
    rows, cols, bins = held.shape
    half = cols // 2
    lanes = lane_index((step * half, LANES))
    low = lanes < bins
    copies = []
    for start in range(0, rows, step):
        code = code_ref[start : start + step].reshape(step * half, LANES)
        code = code.astype(jnp.int32).astype(jnp.float32)
        power = jnp.sum(jnp.where(lanes == bins - 1, code, 0.0), axis=1, keepdims=True)
        other = code * (jnp.exp2(power) * (1.0 / CODE_TOP))
        other = jnp.where(lanes % bins == bins - 1, 0.0, other)
        at = pl.ds((part * rows + start) * half, step * half)
        for side, own_ref in enumerate((first_ref, second_ref)):
            mirrored = other if side == 0 else pltpu.roll(other, bins, 1)
            logits = jnp.where(low, own_ref[at, :] + mirrored, -jnp.inf)
            top = jnp.max(logits, axis=1, keepdims=True)
            raised = jnp.exp(logits - top)
            share = raised * (1.0 / jnp.sum(raised, axis=1, keepdims=True))
            held[start : start + step, side * half : (side + 1) * half, :] = share[
                :, :bins
            ].reshape(step, half, bins)
        copies.append(
            pltpu.make_async_copy(
                held.at[pl.ds(start, step)],
                out_ref.at[pl.ds(part * rows + start, step)],
                sems.at[start // step],
            )
        )
        copies[-1].start()
    for copy in copies:
        copy.wait()


def attention_kernel(
    bins,
    single_ref,
    keys_ref,
    mask_ref,
    gain_ref,
    in_ref,
    first_ref,
    second_ref,
    part_ref,
    gates_ref,
    scores,
):
    rows, width = single_ref.shape
    heads, cols = scores.shape[1:]
    head_width = width // heads
    half = cols // 2
    gain = gain_ref[...].reshape(1, -1)
    query_inner = (centered(single_ref[...].astype(jnp.float32)) * gain).astype(jnp.bfloat16)
    key_inner = (centered(keys_ref[...].astype(jnp.float32)) * gain).astype(jnp.bfloat16)
    queries = dot(query_inner, in_ref[:, :width]) * (1.0 / math.sqrt(head_width))
    gates_ref[...] = jax.nn.sigmoid(dot(query_inner, in_ref[:, 3 * width :]))
    keys_proj = dot(key_inner, in_ref[:, width : 2 * width]).astype(jnp.bfloat16)
    values_proj = dot(key_inner, in_ref[:, 2 * width : 3 * width]).astype(jnp.bfloat16)
    shape = (heads, width)
    lane = lane_index(shape)
    head = lax.broadcasted_iota(jnp.int32, shape, 0)
    own_head = jnp.where((lane >= head * head_width) & (lane < (head + 1) * head_width), 1.0, 0.0)
    spread = (queries[:, None, :] * own_head[None]).astype(jnp.bfloat16)
    scores[...] = dot_t(spread.reshape(rows * heads, width), keys_proj).reshape(rows, heads, cols)
    shape = (heads, 2 * LANES)
    lane = lane_index(shape) % LANES
    pick = (lane == lax.broadcasted_iota(jnp.int32, shape, 0) + bins).astype(jnp.bfloat16)
    for row in range(rows):
        block = jnp.concatenate(
            [ref[row * half : (row + 1) * half, :] for ref in (first_ref, second_ref)], axis=0
        )
        scores[row] += dot_t(pick, jnp.concatenate(split(block), axis=1))
    kept = jnp.where(mask_ref[...].reshape(1, -1) > 0, scores[...].reshape(rows * heads, cols), -1000000000.0)
    top = jnp.max(kept, axis=-1, keepdims=True)
    weights = jnp.exp(kept - top)
    total = jnp.sum(weights, axis=-1, keepdims=True)
    summed = dot((weights * (1.0 / total)).astype(jnp.bfloat16), values_proj)
    summed = jnp.sum(summed.reshape(rows, heads, width) * own_head[None], axis=1)
    part_ref[:, :width] = summed.astype(jnp.bfloat16)
    level = top + jnp.log(total)
    high = level.astype(jnp.bfloat16).astype(jnp.float32)
    middle = (level - high).astype(jnp.bfloat16).astype(jnp.float32)
    low = level - high - middle
    shape = (heads, LANES)
    lane = lane_index(shape)
    head = lax.broadcasted_iota(jnp.int32, shape, 0)
    spread = jnp.zeros((rows, heads, LANES), jnp.float32)
    for place, piece in enumerate((high, middle, low)):
        at = (lane == head + place * heads).astype(jnp.float32)
        spread += piece.reshape(rows, heads, 1) * at[None]
    part_ref[:, width:] = jnp.sum(spread, axis=1).astype(jnp.bfloat16)


def joined_kernel(heads, count, *refs):
    parts, (gates_ref, out_weight_ref, out_ref, held, sem) = refs[:count], refs[count:]
    width = gates_ref.shape[1]
    head_width = width // heads
    shape = (LANES, width)
    lane = lane_index(shape)
    row = lax.broadcasted_iota(jnp.int32, shape, 0)
    head = row % heads
    spread = (
        (lane >= head * head_width) & (lane < (head + 1) * head_width) & (row < 3 * heads)
    ).astype(jnp.bfloat16)
    levels = [dot(part[:, width:], spread) for part in parts]
    top = functools.reduce(jnp.maximum, levels)
    total, summed = 0.0, 0.0
    for level, part in zip(levels, parts):
        factor = jnp.exp(level - top)
        total += factor
        summed += factor * part[:, :width].astype(jnp.float32)
    gated = (gates_ref[...] * (summed / total)).astype(jnp.bfloat16)
    held[...] = dot(gated, out_weight_ref[...]).astype(jnp.bfloat16)
    copy = pltpu.make_async_copy(held, out_ref, sem)
    copy.start()
    copy.wait()


def body(
    row_count,
    col_count,
    pair,
    single,
    token_mask,
    pair_gain,
    transition_in,
    transition_out,
    bias_weight,
    bin_weight,
    single_gain,
    attention_in,
    attention_out,
):
    rows, cols, channels = pair.shape
    width = single.shape[1]
    heads, bins = bias_weight.shape[1], bin_weight.shape[1]
    hidden = transition_out.shape[0]
    half = cols // 2
    mirror = [
        (r * col_count + c, c * col_count + r) for r in range(row_count) for c in range(col_count)
    ]

    key_pairs = [
        (c * col_count + (r + col_count // 2) % col_count, r * col_count + c)
        for r in range(row_count)
        for c in range(col_count)
    ]

    def mirrored(value, pairs=mirror):
        return lax.ppermute(value, ("row", "col"), pairs)

    bf16, f32, i16 = jnp.bfloat16, jnp.float32, jnp.int16
    heads_out = near((rows * half, LANES), f32)
    first, code, later, *kept = call(
        first_kernel,
        (
            heads_out,
            near((half, rows // 2, LANES), i16),
            near((rows, half, channels), bf16),
            near(pair_gain.shape, f32),
            near(transition_in.shape, bf16),
            near((hidden + channels, 2 * LANES), bf16),
        ),
        (pair, pair_gain, transition_in, transition_out, bias_weight.T, bin_weight.T),
        scratch=(
            pltpu.VMEM((rows, half, channels), bf16),
            pltpu.VMEM(transition_out.shape, bf16),
            pltpu.VMEM((heads, channels), f32),
            pltpu.VMEM((bins, channels), f32),
            pltpu.VMEM((LANES, channels), f32),
            pltpu.SemaphoreType.DMA((7,)),
        ),
        far=range(6),
    )
    received = [mirrored(code)]
    behind, _ = lax.optimization_barrier((single, code))
    keys = mirrored(behind, key_pairs)
    second, code = call(
        functools.partial(second_kernel, bins),
        (heads_out, near((half, rows // 2, LANES), i16)),
        (later, *kept),
    )
    own = (first, second)
    code, keys = lax.optimization_barrier((code, keys))
    received.append(mirrored(code))
    part_sums, gates = call(
        functools.partial(attention_kernel, bins),
        (
            near((rows, width + LANES), jnp.bfloat16),
            near((rows, width), jnp.float32),
        ),
        (single, keys, token_mask, single_gain, attention_in, *own),
        scratch=(pltpu.VMEM((rows, heads, cols), jnp.float32),),
    )
    parts = [part_sums]
    for away in range(1, col_count):
        ring = [(c, (c + away) % col_count) for c in range(col_count)]
        parts.append(lax.ppermute(part_sums, "col", ring))
    distogram = None
    count = rows // 2
    for part in range(2):
        distogram = call(
            functools.partial(softmax_kernel, part, SOFT_STEP),
            jax.ShapeDtypeStruct((rows, cols, bins), jnp.float32),
            (*own, received[part]) + ((distogram,) if part else ()),
            scratch=(
                pltpu.VMEM((count, cols, bins), jnp.float32),
                pltpu.SemaphoreType.DMA((count // SOFT_STEP,)),
            ),
            far=(3,) if part else (),
            aliases={3: 0} if part else {},
        )
        if part == 0:
            *parts, distogram = lax.optimization_barrier((*parts, distogram))
            single_update = call(
                functools.partial(joined_kernel, heads, col_count),
                jax.ShapeDtypeStruct((rows, width), bf16),
                (*parts, gates, attention_out),
                scratch=(pltpu.VMEM((rows, width), bf16), pltpu.SemaphoreType.DMA),
            )
    return (distogram, single_update)


def solution(mesh):
    in_specs = (
        P(("groups", "row"), "col", None),
        P(("groups", "row"), None),
        P(("groups", "col")),
        P(),
        P(),
        P(),
        P(),
        P(),
        P(),
        P(),
        P(),
    )
    out_specs = (P(("groups", "row"), "col", None), P(("groups", "row"), None))
    own = functools.partial(body, mesh.shape["row"], mesh.shape["col"])
    return jax.shard_map(own, mesh=mesh, in_specs=in_specs, out_specs=out_specs, check_vma=False)
```

```python
import functools
import math

import jax
import jax.numpy as jnp
from jax import lax
from jax.experimental import pallas as pl
from jax.experimental.pallas import tpu as pltpu
from jax.sharding import PartitionSpec as P

LANES = 128
CODE_TOP = 32767.0
PAIR_STEP = 8
CODE_GROUP = 8
SOFT_STEP = 16
VMEM_LIMIT = 56 * 1024 * 1024


def near(shape, dtype):
    return pltpu.VMEM(shape, dtype)


def call(kernel, outs, args, scratch=(), far=(), aliases=None):
    def out_spec(out):
        inside = isinstance(out, type(near((8, LANES), jnp.float32)))
        return pl.BlockSpec(memory_space=pltpu.VMEM if inside else pl.ANY)

    return pl.pallas_call(
        kernel,
        out_shape=outs,
        in_specs=[
            pl.BlockSpec(memory_space=pl.ANY if k in far else pltpu.VMEM) for k in range(len(args))
        ],
        out_specs=jax.tree.map(out_spec, outs),
        scratch_shapes=list(scratch),
        input_output_aliases=aliases or {},
        compiler_params=pltpu.CompilerParams(vmem_limit_bytes=VMEM_LIMIT),
    )(
        *[
            a if k in far else pltpu.with_memory_space_constraint(a, pltpu.VMEM)
            for k, a in enumerate(args)
        ]
    )


def centered(values):
    rest = values - jnp.mean(values, axis=-1, keepdims=True)
    variance = jnp.mean(rest * rest, axis=-1, keepdims=True)
    return rest * lax.rsqrt(variance + 1e-05)


def dot(a, b):
    return jnp.dot(a, b, preferred_element_type=jnp.float32)


def dot_t(a, b):
    return lax.dot_general(a, b, (((1,), (1,)), ((), ())), preferred_element_type=jnp.float32)


def split(value):
    high = value.astype(jnp.bfloat16)
    return high, (value - high.astype(jnp.float32)).astype(jnp.bfloat16)


def lane_index(shape):
    return lax.broadcasted_iota(jnp.int32, shape, len(shape) - 1)


def fill_weights(out_ref, bias_ref, bin_ref, flat_weight, weight_ref):
    bins, heads = bin_ref.shape[0], bias_ref.shape[0]
    hidden = out_ref.shape[0]
    flat_weight[...] = jnp.zeros_like(flat_weight)
    flat_weight[:bins, :] = bin_ref[...] - bin_ref[bins - 1 :, :]
    flat_weight[bins : bins + heads, :] = bias_ref[...]
    weight = flat_weight[...].T
    high = weight.astype(jnp.bfloat16)
    rest = weight - high.astype(jnp.float32)
    middle = rest.astype(jnp.bfloat16)
    low = (rest - middle.astype(jnp.float32)).astype(jnp.bfloat16)
    parts = dot(out_ref[...], jnp.concatenate([high, middle, low], axis=1))
    folded = parts[:, :LANES] + parts[:, LANES : 2 * LANES] + parts[:, 2 * LANES :]
    folded_high, folded_low = split(folded)
    weight_ref[:hidden, :LANES] = folded_high
    weight_ref[:hidden, LANES:] = folded_low
    weight_ref[hidden:, :LANES] = high
    weight_ref[hidden:, LANES:] = middle


def pair_heads(pair_ref, gain, in_ref, weight_ref, heads_ref):
    rows, cols, channels = pair_ref.shape
    hidden = in_ref.shape[1] // 2
    for start in range(0, rows, PAIR_STEP):
        tokens = pair_ref[start : start + PAIR_STEP].reshape(PAIR_STEP * cols, channels)
        inner = centered(tokens.astype(jnp.float32)) * gain
        both = dot(inner.astype(jnp.bfloat16), in_ref[...])
        gate = both[:, :hidden] * 0.5
        gated = (gate * (1.0 + jnp.tanh(gate)) * both[:, hidden:]).astype(jnp.bfloat16)
        twice = dot(gated, weight_ref[:hidden, :]) + dot(tokens, weight_ref[hidden:, :])
        at = slice(start * cols, (start + PAIR_STEP) * cols)
        heads_ref[at, :] = twice[:, :LANES] + twice[:, LANES:]


def fill_code(bins, rows, cols, heads_ref, code_ref):
    half = rows // 2
    lanes = lane_index((half * CODE_GROUP, LANES))
    for start in range(0, cols, CODE_GROUP):
        first, second = (
            jnp.concatenate(
                [
                    heads_ref[pl.ds(top * cols + col, half, stride=cols), :]
                    for col in range(start, start + CODE_GROUP)
                ],
                axis=0,
            )
            for top in (0, half)
        )
        packed = jnp.where(lanes < bins, first, pltpu.roll(second, bins, 1))
        top = jnp.max(jnp.abs(packed), axis=1, keepdims=True)
        power = jnp.ceil(jnp.log2(jnp.maximum(top, 1e-30)))
        code = jnp.where(
            lanes % bins == bins - 1, power, packed * (jnp.exp2(-power) * CODE_TOP)
        )
        code = jnp.round(code).astype(jnp.int32).astype(jnp.int16)
        code_ref[start : start + CODE_GROUP] = code.reshape(CODE_GROUP, half, LANES)


def first_kernel(
    pair_ref,
    gain_ref,
    in_ref,
    out_ref,
    bias_ref,
    bin_ref,
    heads_ref,
    code_ref,
    later_ref,
    gain_near,
    in_near,
    weight_ref,
    tile,
    out_near,
    bias_near,
    bin_near,
    flat_weight,
    sems,
):
    rows, cols, _ = tile.shape

    def bring(source, target, sem):
        copy = pltpu.make_async_copy(source, target, sem)
        copy.start()
        return copy

    small = [
        bring(source, target, sems.at[k])
        for k, (source, target) in enumerate(
            ((bias_ref, bias_near), (bin_ref, bin_near), (out_ref, out_near))
        )
    ]
    gain_copy = bring(gain_ref, gain_near, sems.at[3])
    tile_copy = bring(pair_ref.at[:, pl.ds(0, cols)], tile, sems.at[4])
    in_copy = bring(in_ref, in_near, sems.at[5])
    later = bring(pair_ref.at[:, pl.ds(cols, cols)], later_ref, sems.at[6])
    for copy in small:
        copy.wait()
    fill_weights(out_near, bias_near, bin_near, flat_weight, weight_ref)
    gain_copy.wait()
    in_copy.wait()
    tile_copy.wait()
    gain = gain_near[...].reshape(1, -1)
    pair_heads(tile, gain, in_near, weight_ref, heads_ref)
    fill_code(bin_ref.shape[0], rows, cols, heads_ref, code_ref)
    later.wait()


def second_kernel(bins, pair_ref, gain_ref, in_ref, weight_ref, heads_ref, code_ref):
    rows, cols, _ = pair_ref.shape
    gain = gain_ref[...].reshape(1, -1)
    pair_heads(pair_ref, gain, in_ref, weight_ref, heads_ref)
    fill_code(bins, rows, cols, heads_ref, code_ref)


def apart(size):
    return size // 2


def softmax_kernel(part, turn, step, size, heads, first_ref, second_ref, code_ref, *refs):
    if turn == 2:
        parts, (gates_ref, weight_ref, _) = refs[:size], refs[size : size + 3]
        out_ref, single_ref, held, sems, single_held, single_sem = refs[size + 3 :]
    else:
        out_ref, held, sems = refs[-3:]
    rows, cols, bins = held.shape
    half = cols // 2
    distance = lax.axis_index("col") - lax.axis_index("row")
    relayed = (distance == apart(size)) | (distance == apart(size) - size)
    lanes = lane_index((step * half, LANES))
    low = lanes < bins

    def work():
        copies = []
        for start in range(0, rows, step):
            code = code_ref[start : start + step]
            if turn == 0:
                code = lax.select_n(distance == 0, code, refs[0][start : start + step])
            code = code.reshape(step * half, LANES)
            code = code.astype(jnp.int32).astype(jnp.float32)
            power = jnp.sum(jnp.where(lanes == bins - 1, code, 0.0), axis=1, keepdims=True)
            other = code * (jnp.exp2(power) * (1.0 / CODE_TOP))
            other = jnp.where(lanes % bins == bins - 1, 0.0, other)
            at = pl.ds((part * rows + start) * half, step * half)
            for side, own_ref in enumerate((first_ref, second_ref)):
                mirrored = other if side == 0 else pltpu.roll(other, bins, 1)
                logits = jnp.where(low, own_ref[at, :] + mirrored, -jnp.inf)
                top = jnp.max(logits, axis=1, keepdims=True)
                raised = jnp.exp(logits - top)
                share = raised * (1.0 / jnp.sum(raised, axis=1, keepdims=True))
                held[start : start + step, side * half : (side + 1) * half, :] = share[
                    :, :bins
                ].reshape(step, half, bins)
            copies.append(
                pltpu.make_async_copy(
                    held.at[pl.ds(start, step)],
                    out_ref.at[pl.ds(part * rows + start, step)],
                    sems.at[start // step],
                )
            )
            copies[-1].start()
        for copy in copies:
            copy.wait()

    if turn == 2:
        single_held[...] = joined(heads, parts, gates_ref, weight_ref)
        single_copy = pltpu.make_async_copy(single_held, single_ref, single_sem)
        single_copy.start()
    if turn == 1:
        work()
    else:
        pl.when(relayed if turn == 2 else jnp.logical_not(relayed))(work)
    if turn == 2:
        single_copy.wait()


def attention_kernel(
    bins,
    single_ref,
    keys_ref,
    mask_ref,
    gain_ref,
    in_ref,
    first_ref,
    second_ref,
    part_ref,
    gates_ref,
    scores,
):
    rows, width = single_ref.shape
    heads, cols = scores.shape[1:]
    head_width = width // heads
    half = cols // 2
    gain = gain_ref[...].reshape(1, -1)
    query_inner = (centered(single_ref[...].astype(jnp.float32)) * gain).astype(jnp.bfloat16)
    key_inner = (centered(keys_ref[...].astype(jnp.float32)) * gain).astype(jnp.bfloat16)
    queries = dot(query_inner, in_ref[:, :width]) * (1.0 / math.sqrt(head_width))
    gates_ref[...] = jax.nn.sigmoid(dot(query_inner, in_ref[:, 3 * width :]))
    keys_proj = dot(key_inner, in_ref[:, width : 2 * width]).astype(jnp.bfloat16)
    values_proj = dot(key_inner, in_ref[:, 2 * width : 3 * width]).astype(jnp.bfloat16)
    shape = (heads, width)
    lane = lane_index(shape)
    head = lax.broadcasted_iota(jnp.int32, shape, 0)
    own_head = jnp.where((lane >= head * head_width) & (lane < (head + 1) * head_width), 1.0, 0.0)
    spread = (queries[:, None, :] * own_head[None]).astype(jnp.bfloat16)
    scores[...] = dot_t(spread.reshape(rows * heads, width), keys_proj).reshape(rows, heads, cols)
    shape = (heads, 2 * LANES)
    lane = lane_index(shape) % LANES
    pick = (lane == lax.broadcasted_iota(jnp.int32, shape, 0) + bins).astype(jnp.bfloat16)
    for row in range(rows):
        block = jnp.concatenate(
            [ref[row * half : (row + 1) * half, :] for ref in (first_ref, second_ref)], axis=0
        )
        scores[row] += dot_t(pick, jnp.concatenate(split(block), axis=1))
    kept = jnp.where(mask_ref[...].reshape(1, -1) > 0, scores[...].reshape(rows * heads, cols), -1000000000.0)
    top = jnp.max(kept, axis=-1, keepdims=True)
    weights = jnp.exp(kept - top)
    total = jnp.sum(weights, axis=-1, keepdims=True)
    summed = dot((weights * (1.0 / total)).astype(jnp.bfloat16), values_proj)
    summed = jnp.sum(summed.reshape(rows, heads, width) * own_head[None], axis=1)
    part_ref[:, :width] = summed.astype(jnp.bfloat16)
    level = top + jnp.log(total)
    high = level.astype(jnp.bfloat16).astype(jnp.float32)
    middle = (level - high).astype(jnp.bfloat16).astype(jnp.float32)
    low = level - high - middle
    shape = (heads, LANES)
    lane = lane_index(shape)
    head = lax.broadcasted_iota(jnp.int32, shape, 0)
    spread = jnp.zeros((rows, heads, LANES), jnp.float32)
    for place, piece in enumerate((high, middle, low)):
        at = (lane == head + place * heads).astype(jnp.float32)
        spread += piece.reshape(rows, heads, 1) * at[None]
    part_ref[:, width:] = jnp.sum(spread, axis=1).astype(jnp.bfloat16)


def joined(heads, parts, gates_ref, out_weight_ref):
    width = gates_ref.shape[1]
    head_width = width // heads
    shape = (LANES, width)
    lane = lane_index(shape)
    row = lax.broadcasted_iota(jnp.int32, shape, 0)
    head = row % heads
    spread = (
        (lane >= head * head_width) & (lane < (head + 1) * head_width) & (row < 3 * heads)
    ).astype(jnp.bfloat16)
    levels = [dot(part[:, width:], spread) for part in parts]
    top = functools.reduce(jnp.maximum, levels)
    total, summed = 0.0, 0.0
    for level, part in zip(levels, parts):
        factor = jnp.exp(level - top)
        total += factor
        summed += factor * part[:, :width].astype(jnp.float32)
    gated = (gates_ref[...] * (summed / total)).astype(jnp.bfloat16)
    return dot(gated, out_weight_ref[...]).astype(jnp.bfloat16)


def body(
    row_count,
    col_count,
    pair,
    single,
    token_mask,
    pair_gain,
    transition_in,
    transition_out,
    bias_weight,
    bin_weight,
    single_gain,
    attention_in,
    attention_out,
):
    rows, cols, channels = pair.shape
    width = single.shape[1]
    heads, bins = bias_weight.shape[1], bin_weight.shape[1]
    hidden = transition_out.shape[0]
    half = cols // 2
    grid = [(r, c) for r in range(row_count) for c in range(col_count)]
    far = [(r, c) for r, c in grid if c == (r + apart(col_count)) % col_count]

    def moved(value, pairs):
        pairs = [(a * col_count + b, c * col_count + d) for (a, b), (c, d) in pairs]
        return lax.ppermute(value, ("row", "col"), pairs)

    mirror = [((r, c), (c, r)) for r, c in grid]
    near_mirror = [((r, c), (c, r)) for r, c in grid if r != c and (r, c) not in far]
    to_relay = [((r, c), (r, r)) for r, c in far]
    from_relay = [((r, r), (c, r)) for r, c in far]
    half_way = [((c, (r + apart(col_count)) % col_count), (r, c)) for r, c in grid]
    bf16, f32, i16 = jnp.bfloat16, jnp.float32, jnp.int16
    heads_out = near((rows * half, LANES), f32)
    first, code, later, *kept = call(
        first_kernel,
        (
            heads_out,
            near((half, rows // 2, LANES), i16),
            near((rows, half, channels), bf16),
            near(pair_gain.shape, f32),
            near(transition_in.shape, bf16),
            near((hidden + channels, 2 * LANES), bf16),
        ),
        (pair, pair_gain, transition_in, transition_out, bias_weight.T, bin_weight.T),
        scratch=(
            pltpu.VMEM((rows, half, channels), bf16),
            pltpu.VMEM(transition_out.shape, bf16),
            pltpu.VMEM((heads, channels), f32),
            pltpu.VMEM((bins, channels), f32),
            pltpu.VMEM((LANES, channels), f32),
            pltpu.SemaphoreType.DMA((7,)),
        ),
        far=range(6),
    )
    own_code, early = code, moved(code, near_mirror + to_relay)
    behind, _ = lax.optimization_barrier((single, code))
    keys = moved(behind, half_way)
    second, code = call(
        functools.partial(second_kernel, bins),
        (heads_out, near((half, rows // 2, LANES), i16)),
        (later, *kept),
    )
    own = (first, second)
    code, keys = lax.optimization_barrier((code, keys))
    direct = moved(code, mirror)
    relayed = moved(early, from_relay)
    part_sums, gates = call(
        functools.partial(attention_kernel, bins),
        (
            near((rows, width + LANES), jnp.bfloat16),
            near((rows, width), jnp.float32),
        ),
        (single, keys, token_mask, single_gain, attention_in, *own),
        scratch=(pltpu.VMEM((rows, heads, cols), jnp.float32),),
    )
    parts = [part_sums]
    for away in range(1, col_count):
        ring = [(c, (c + away) % col_count) for c in range(col_count)]
        parts.append(lax.ppermute(part_sums, "col", ring))
    count = rows // 2
    distogram_out = jax.ShapeDtypeStruct((rows, cols, bins), f32)
    single_out = jax.ShapeDtypeStruct((rows, width), bf16)
    scratch = (pltpu.VMEM((count, cols, bins), f32), pltpu.SemaphoreType.DMA((count // SOFT_STEP,)))

    def turn(number, part, codes, outs, more=(), scratch=scratch):
        last = 2 + len(codes) + len(more) - 1
        return call(
            functools.partial(softmax_kernel, part, number, SOFT_STEP, col_count, heads),
            outs,
            (*own, *codes, *more),
            scratch=scratch,
            far=(last,) if number else (),
            aliases={last: 0} if number else {},
        )

    distogram = turn(0, 0, (early, own_code), distogram_out)
    distogram = turn(1, 1, (direct,), distogram_out, (distogram,))
    distogram, single_update = turn(
        2,
        0,
        (relayed,),
        (distogram_out, single_out),
        (*parts, gates, attention_out, distogram),
        scratch=(*scratch, pltpu.VMEM((rows, width), bf16), pltpu.SemaphoreType.DMA),
    )
    return (distogram, single_update)


def solution(mesh):
    in_specs = (
        P(("groups", "row"), "col", None),
        P(("groups", "row"), None),
        P(("groups", "col")),
        P(),
        P(),
        P(),
        P(),
        P(),
        P(),
        P(),
        P(),
    )
    out_specs = (P(("groups", "row"), "col", None), P(("groups", "row"), None))
    own = functools.partial(body, mesh.shape["row"], mesh.shape["col"])
    return jax.shard_map(own, mesh=mesh, in_specs=in_specs, out_specs=out_specs, check_vma=False)
```

```python
import functools
import math

import jax
import jax.numpy as jnp
from jax import lax
from jax.experimental import pallas as pl
from jax.experimental.pallas import tpu as pltpu
from jax.sharding import PartitionSpec as P

LANES = 128
CODE_TOP = 32767.0
PAIR_STEP = 8
CODE_GROUP = 8
SOFT_STEP = 16
ROW_TILE = 8
VMEM_LIMIT = 56 * 1024 * 1024


def near(shape, dtype):
    return pltpu.VMEM(shape, dtype)


def call(kernel, outs, args, scratch=(), far=(), aliases=None):
    def out_spec(out):
        inside = isinstance(out, type(near((8, LANES), jnp.float32)))
        return pl.BlockSpec(memory_space=pltpu.VMEM if inside else pl.ANY)

    return pl.pallas_call(
        kernel,
        out_shape=outs,
        in_specs=[
            pl.BlockSpec(memory_space=pl.ANY if k in far else pltpu.VMEM) for k in range(len(args))
        ],
        out_specs=jax.tree.map(out_spec, outs),
        scratch_shapes=list(scratch),
        input_output_aliases=aliases or {},
        compiler_params=pltpu.CompilerParams(vmem_limit_bytes=VMEM_LIMIT),
    )(
        *[
            a if k in far else pltpu.with_memory_space_constraint(a, pltpu.VMEM)
            for k, a in enumerate(args)
        ]
    )


def centered(values):
    rest = values - jnp.mean(values, axis=-1, keepdims=True)
    variance = jnp.mean(rest * rest, axis=-1, keepdims=True)
    return rest * lax.rsqrt(variance + 1e-05)


def dot(a, b):
    return jnp.dot(a, b, preferred_element_type=jnp.float32)


def dot_t(a, b):
    return lax.dot_general(a, b, (((1,), (1,)), ((), ())), preferred_element_type=jnp.float32)


def split(value):
    high = value.astype(jnp.bfloat16)
    return high, (value - high.astype(jnp.float32)).astype(jnp.bfloat16)


def lane_index(shape):
    return lax.broadcasted_iota(jnp.int32, shape, len(shape) - 1)


def fill_weights(out_ref, bias_ref, bin_ref, flat_weight, weight_ref):
    bins, heads = bin_ref.shape[0], bias_ref.shape[0]
    hidden = out_ref.shape[0]
    flat_weight[...] = jnp.zeros_like(flat_weight)
    flat_weight[:bins, :] = bin_ref[...] - bin_ref[bins - 1 :, :]
    flat_weight[bins : bins + heads, :] = bias_ref[...]
    weight = flat_weight[...].T
    high = weight.astype(jnp.bfloat16)
    rest = weight - high.astype(jnp.float32)
    middle = rest.astype(jnp.bfloat16)
    low = (rest - middle.astype(jnp.float32)).astype(jnp.bfloat16)
    parts = dot(out_ref[...], jnp.concatenate([high, middle, low], axis=1))
    folded = parts[:, :LANES] + parts[:, LANES : 2 * LANES] + parts[:, 2 * LANES :]
    folded_high, folded_low = split(folded)
    weight_ref[:hidden, :LANES] = folded_high
    weight_ref[:hidden, LANES:] = folded_low
    weight_ref[hidden:, :LANES] = high
    weight_ref[hidden:, LANES:] = middle


def pair_heads(pair_ref, gain, in_ref, weight_ref, heads_ref):
    rows, cols, channels = pair_ref.shape
    hidden = in_ref.shape[1] // 2
    for start in range(0, rows, PAIR_STEP):
        tokens = pair_ref[start : start + PAIR_STEP].reshape(PAIR_STEP * cols, channels)
        inner = centered(tokens.astype(jnp.float32)) * gain
        both = dot(inner.astype(jnp.bfloat16), in_ref[...])
        gate = both[:, :hidden] * 0.5
        gated = (gate * (1.0 + jnp.tanh(gate)) * both[:, hidden:]).astype(jnp.bfloat16)
        twice = dot(gated, weight_ref[:hidden, :]) + dot(tokens, weight_ref[hidden:, :])
        at = slice(start * cols, (start + PAIR_STEP) * cols)
        heads_ref[at, :] = twice[:, :LANES] + twice[:, LANES:]


def fill_code(bins, rows, cols, heads_ref, code_ref):
    half = rows // 2
    lanes = lane_index((half * CODE_GROUP, LANES))
    for start in range(0, cols, CODE_GROUP):
        first, second = (
            jnp.concatenate(
                [
                    heads_ref[pl.ds(top * cols + col, half, stride=cols), :]
                    for col in range(start, start + CODE_GROUP)
                ],
                axis=0,
            )
            for top in (0, half)
        )
        packed = jnp.where(lanes < bins, first, pltpu.roll(second, bins, 1))
        top = jnp.max(jnp.abs(packed), axis=1, keepdims=True)
        power = jnp.ceil(jnp.log2(jnp.maximum(top, 1e-30)))
        code = jnp.where(
            lanes % bins == bins - 1, power, packed * (jnp.exp2(-power) * CODE_TOP)
        )
        code = jnp.round(code).astype(jnp.int32).astype(jnp.int16)
        code_ref[start : start + CODE_GROUP] = code.reshape(CODE_GROUP, half, LANES)


def first_kernel(
    pair_ref,
    gain_ref,
    in_ref,
    out_ref,
    bias_ref,
    bin_ref,
    heads_ref,
    code_ref,
    later_ref,
    gain_near,
    in_near,
    weight_ref,
    tile,
    out_near,
    bias_near,
    bin_near,
    flat_weight,
    sems,
):
    rows, cols, _ = tile.shape

    def bring(source, target, sem):
        copy = pltpu.make_async_copy(source, target, sem)
        copy.start()
        return copy

    small = [
        bring(source, target, sems.at[k])
        for k, (source, target) in enumerate(
            ((bias_ref, bias_near), (bin_ref, bin_near), (out_ref, out_near))
        )
    ]
    gain_copy = bring(gain_ref, gain_near, sems.at[3])
    tile_copy = bring(pair_ref.at[:, pl.ds(0, cols)], tile, sems.at[4])
    in_copy = bring(in_ref, in_near, sems.at[5])
    later = bring(pair_ref.at[:, pl.ds(cols, later_ref.shape[1])], later_ref, sems.at[6])
    for copy in small:
        copy.wait()
    fill_weights(out_near, bias_near, bin_near, flat_weight, weight_ref)
    gain_copy.wait()
    in_copy.wait()
    tile_copy.wait()
    gain = gain_near[...].reshape(1, -1)
    pair_heads(tile, gain, in_near, weight_ref, heads_ref)
    fill_code(bin_ref.shape[0], rows, cols, heads_ref, code_ref)
    later.wait()


def second_kernel(bins, pair_ref, gain_ref, in_ref, weight_ref, heads_ref, code_ref):
    rows, cols, _ = pair_ref.shape
    gain = gain_ref[...].reshape(1, -1)
    pair_heads(pair_ref, gain, in_ref, weight_ref, heads_ref)
    fill_code(bins, rows, cols, heads_ref, code_ref)


def apart(size):
    return size // 2


def softmax_kernel(part, turn, most, size, heads, first_ref, second_ref, code_ref, *refs):
    if turn == 2:
        parts, (gates_ref, weight_ref, _) = refs[:size], refs[size : size + 3]
        out_ref, single_ref, held, sems, single_held, single_sem = refs[size + 3 :]
    else:
        out_ref, held, sems = refs[-3:]
    rows, cols, bins = held.shape
    half = cols // 2
    distance = lax.axis_index("col") - lax.axis_index("row")
    relayed = (distance == apart(size)) | (distance == apart(size) - size)
    begin = first_ref.shape[1] if part else 0

    def own(side, at):
        cut = first_ref.shape[1]
        low, high = side * half, (side + 1) * half
        pieces = []
        if low < cut:
            pieces.append(first_ref[at, low : min(high, cut)])
        if high > cut:
            pieces.append(second_ref[at, max(low - cut, 0) : high - cut])
        return jnp.concatenate(pieces, axis=1).reshape(-1, LANES)

    def work():
        copies = []
        for start in range(0, rows, most):
            step = min(most, rows - start)
            lanes = lane_index((step * half, LANES))
            low = lanes < bins
            code = code_ref[start : start + step]
            if turn == 0:
                code = lax.select_n(distance == 0, code, refs[0][start : start + step])
            code = code.reshape(step * half, LANES)
            code = code.astype(jnp.int32).astype(jnp.float32)
            power = jnp.sum(jnp.where(lanes == bins - 1, code, 0.0), axis=1, keepdims=True)
            other = code * (jnp.exp2(power) * (1.0 / CODE_TOP))
            other = jnp.where(lanes % bins == bins - 1, 0.0, other)
            at = slice(begin + start, begin + start + step)
            for side in range(2):
                mirrored = other if side == 0 else pltpu.roll(other, bins, 1)
                logits = jnp.where(low, own(side, at) + mirrored, -jnp.inf)
                top = jnp.max(logits, axis=1, keepdims=True)
                raised = jnp.exp(logits - top)
                share = raised * (1.0 / jnp.sum(raised, axis=1, keepdims=True))
                held[start : start + step, side * half : (side + 1) * half, :] = share[
                    :, :bins
                ].reshape(step, half, bins)
            copies.append(
                pltpu.make_async_copy(
                    held.at[pl.ds(start, step)],
                    out_ref.at[pl.ds(begin + start, step)],
                    sems.at[start // most],
                )
            )
            copies[-1].start()
        for copy in copies:
            copy.wait()

    if turn == 2:
        single_held[...] = joined(heads, parts, gates_ref, weight_ref)
        single_copy = pltpu.make_async_copy(single_held, single_ref, single_sem)
        single_copy.start()
    if turn == 1:
        work()
    else:
        pl.when(relayed if turn == 2 else jnp.logical_not(relayed))(work)
    if turn == 2:
        single_copy.wait()


def attention_kernel(
    bins,
    single_ref,
    keys_ref,
    mask_ref,
    gain_ref,
    in_ref,
    first_ref,
    second_ref,
    part_ref,
    gates_ref,
    scores,
):
    rows, width = single_ref.shape
    heads, cols = scores.shape[1:]
    head_width = width // heads
    gain = gain_ref[...].reshape(1, -1)
    query_inner = (centered(single_ref[...].astype(jnp.float32)) * gain).astype(jnp.bfloat16)
    key_inner = (centered(keys_ref[...].astype(jnp.float32)) * gain).astype(jnp.bfloat16)
    queries = dot(query_inner, in_ref[:, :width]) * (1.0 / math.sqrt(head_width))
    gates_ref[...] = jax.nn.sigmoid(dot(query_inner, in_ref[:, 3 * width :]))
    keys_proj = dot(key_inner, in_ref[:, width : 2 * width]).astype(jnp.bfloat16)
    values_proj = dot(key_inner, in_ref[:, 2 * width : 3 * width]).astype(jnp.bfloat16)
    shape = (heads, width)
    lane = lane_index(shape)
    head = lax.broadcasted_iota(jnp.int32, shape, 0)
    own_head = jnp.where((lane >= head * head_width) & (lane < (head + 1) * head_width), 1.0, 0.0)
    spread = (queries[:, None, :] * own_head[None]).astype(jnp.bfloat16)
    scores[...] = dot_t(spread.reshape(rows * heads, width), keys_proj).reshape(rows, heads, cols)
    shape = (heads, 2 * LANES)
    lane = lane_index(shape) % LANES
    pick = (lane == lax.broadcasted_iota(jnp.int32, shape, 0) + bins).astype(jnp.bfloat16)
    for row in range(rows):
        block = jnp.concatenate(
            [first_ref[row], second_ref[row]], axis=0
        )
        scores[row] += dot_t(pick, jnp.concatenate(split(block), axis=1))
    kept = jnp.where(mask_ref[...].reshape(1, -1) > 0, scores[...].reshape(rows * heads, cols), -1000000000.0)
    top = jnp.max(kept, axis=-1, keepdims=True)
    weights = jnp.exp(kept - top)
    total = jnp.sum(weights, axis=-1, keepdims=True)
    summed = dot((weights * (1.0 / total)).astype(jnp.bfloat16), values_proj)
    summed = jnp.sum(summed.reshape(rows, heads, width) * own_head[None], axis=1)
    part_ref[:, :width] = summed.astype(jnp.bfloat16)
    level = top + jnp.log(total)
    high = level.astype(jnp.bfloat16).astype(jnp.float32)
    middle = (level - high).astype(jnp.bfloat16).astype(jnp.float32)
    low = level - high - middle
    shape = (heads, LANES)
    lane = lane_index(shape)
    head = lax.broadcasted_iota(jnp.int32, shape, 0)
    spread = jnp.zeros((rows, heads, LANES), jnp.float32)
    for place, piece in enumerate((high, middle, low)):
        at = (lane == head + place * heads).astype(jnp.float32)
        spread += piece.reshape(rows, heads, 1) * at[None]
    part_ref[:, width:] = jnp.sum(spread, axis=1).astype(jnp.bfloat16)


def joined(heads, parts, gates_ref, out_weight_ref):
    width = gates_ref.shape[1]
    head_width = width // heads
    shape = (LANES, width)
    lane = lane_index(shape)
    row = lax.broadcasted_iota(jnp.int32, shape, 0)
    head = row % heads
    spread = (
        (lane >= head * head_width) & (lane < (head + 1) * head_width) & (row < 3 * heads)
    ).astype(jnp.bfloat16)
    levels = [dot(part[:, width:], spread) for part in parts]
    top = functools.reduce(jnp.maximum, levels)
    total, summed = 0.0, 0.0
    for level, part in zip(levels, parts):
        factor = jnp.exp(level - top)
        total += factor
        summed += factor * part[:, :width].astype(jnp.float32)
    gated = (gates_ref[...] * (summed / total)).astype(jnp.bfloat16)
    return dot(gated, out_weight_ref[...]).astype(jnp.bfloat16)


def body(
    row_count,
    col_count,
    pair,
    single,
    token_mask,
    pair_gain,
    transition_in,
    transition_out,
    bias_weight,
    bin_weight,
    single_gain,
    attention_in,
    attention_out,
):
    rows, cols, channels = pair.shape
    width = single.shape[1]
    heads, bins = bias_weight.shape[1], bin_weight.shape[1]
    hidden = transition_out.shape[0]
    cut = cols * 5 // 8 // ROW_TILE * ROW_TILE
    rest = cols - cut
    grid = [(r, c) for r in range(row_count) for c in range(col_count)]
    far = [(r, c) for r, c in grid if c == (r + apart(col_count)) % col_count]

    def moved(value, pairs):
        pairs = [(a * col_count + b, c * col_count + d) for (a, b), (c, d) in pairs]
        return lax.ppermute(value, ("row", "col"), pairs)

    mirror = [((r, c), (c, r)) for r, c in grid]
    near_mirror = [((r, c), (c, r)) for r, c in grid if r != c and (r, c) not in far]
    to_relay = [((r, c), (r, r)) for r, c in far]
    from_relay = [((r, r), (c, r)) for r, c in far]
    half_way = [((c, (r + apart(col_count)) % col_count), (r, c)) for r, c in grid]
    bf16, f32, i16 = jnp.bfloat16, jnp.float32, jnp.int16
    first, code, later, *kept = call(
        first_kernel,
        (
            near((rows * cut, LANES), f32),
            near((cut, rows // 2, LANES), i16),
            near((rows, rest, channels), bf16),
            near(pair_gain.shape, f32),
            near(transition_in.shape, bf16),
            near((hidden + channels, 2 * LANES), bf16),
        ),
        (pair, pair_gain, transition_in, transition_out, bias_weight.T, bin_weight.T),
        scratch=(
            pltpu.VMEM((rows, cut, channels), bf16),
            pltpu.VMEM(transition_out.shape, bf16),
            pltpu.VMEM((heads, channels), f32),
            pltpu.VMEM((bins, channels), f32),
            pltpu.VMEM((LANES, channels), f32),
            pltpu.SemaphoreType.DMA((7,)),
        ),
        far=range(6),
    )
    own_code, early = code, moved(code, near_mirror + to_relay)
    behind, _ = lax.optimization_barrier((single, code))
    keys = moved(behind, half_way)
    second, code = call(
        functools.partial(second_kernel, bins),
        (near((rows * rest, LANES), f32), near((rest, rows // 2, LANES), i16)),
        (later, *kept),
    )
    own = (first.reshape(rows, cut, LANES), second.reshape(rows, rest, LANES))
    code, keys = lax.optimization_barrier((code, keys))
    direct = moved(code, mirror)
    passed, _ = lax.optimization_barrier((early, code))
    relayed = moved(passed, from_relay)
    part_sums, gates = call(
        functools.partial(attention_kernel, bins),
        (
            near((rows, width + LANES), jnp.bfloat16),
            near((rows, width), jnp.float32),
        ),
        (single, keys, token_mask, single_gain, attention_in, *own),
        scratch=(pltpu.VMEM((rows, heads, cols), jnp.float32),),
    )
    parts = [part_sums]
    for away in range(1, col_count):
        ring = [(c, (c + away) % col_count) for c in range(col_count)]
        parts.append(lax.ppermute(part_sums, "col", ring))
    distogram_out = jax.ShapeDtypeStruct((rows, cols, bins), f32)
    single_out = jax.ShapeDtypeStruct((rows, width), bf16)

    def turn(number, part, codes, outs, more=(), scratch=()):
        count = codes[0].shape[0]
        blocks = -(-count // SOFT_STEP)
        scratch = (
            pltpu.VMEM((count, cols, bins), f32),
            pltpu.SemaphoreType.DMA((blocks,)),
            *scratch,
        )
        last = 2 + len(codes) + len(more) - 1
        return call(
            functools.partial(softmax_kernel, part, number, SOFT_STEP, col_count, heads),
            outs,
            (*own, *codes, *more),
            scratch=scratch,
            far=(last,) if number else (),
            aliases={last: 0} if number else {},
        )

    distogram = turn(0, 0, (early, own_code), distogram_out)
    distogram = turn(1, 1, (direct,), distogram_out, (distogram,))
    distogram, single_update = turn(
        2,
        0,
        (relayed,),
        (distogram_out, single_out),
        (*parts, gates, attention_out, distogram),
        scratch=(pltpu.VMEM((rows, width), bf16), pltpu.SemaphoreType.DMA),
    )
    return (distogram, single_update)


def solution(mesh):
    in_specs = (
        P(("groups", "row"), "col", None),
        P(("groups", "row"), None),
        P(("groups", "col")),
        P(),
        P(),
        P(),
        P(),
        P(),
        P(),
        P(),
        P(),
    )
    out_specs = (P(("groups", "row"), "col", None), P(("groups", "row"), None))
    own = functools.partial(body, mesh.shape["row"], mesh.shape["col"])
    return jax.shard_map(own, mesh=mesh, in_specs=in_specs, out_specs=out_specs, check_vma=False)
```

```python
import functools
import math

import jax
import jax.numpy as jnp
from jax import lax
from jax.experimental import pallas as pl
from jax.experimental.pallas import tpu as pltpu
from jax.sharding import PartitionSpec as P

LANES = 128
CODE_TOP = 32767.0
PAIR_STEP = 8
CODE_GROUP = 8
SOFT_STEP = 16
ROW_TILE = 8
VMEM_LIMIT = 56 * 1024 * 1024


def near(shape, dtype):
    return pltpu.VMEM(shape, dtype)


def call(kernel, outs, args, scratch=(), far=(), aliases=None):
    def out_spec(out):
        inside = isinstance(out, type(near((8, LANES), jnp.float32)))
        return pl.BlockSpec(memory_space=pltpu.VMEM if inside else pl.ANY)

    return pl.pallas_call(
        kernel,
        out_shape=outs,
        in_specs=[
            pl.BlockSpec(memory_space=pl.ANY if k in far else pltpu.VMEM) for k in range(len(args))
        ],
        out_specs=jax.tree.map(out_spec, outs),
        scratch_shapes=list(scratch),
        input_output_aliases=aliases or {},
        compiler_params=pltpu.CompilerParams(vmem_limit_bytes=VMEM_LIMIT),
    )(
        *[
            a if k in far else pltpu.with_memory_space_constraint(a, pltpu.VMEM)
            for k, a in enumerate(args)
        ]
    )


def centered(values):
    rest = values - jnp.mean(values, axis=-1, keepdims=True)
    variance = jnp.mean(rest * rest, axis=-1, keepdims=True)
    return rest * lax.rsqrt(variance + 1e-05)


def dot(a, b):
    return jnp.dot(a, b, preferred_element_type=jnp.float32)


def dot_t(a, b):
    return lax.dot_general(a, b, (((1,), (1,)), ((), ())), preferred_element_type=jnp.float32)


def split(value):
    high = value.astype(jnp.bfloat16)
    return high, (value - high.astype(jnp.float32)).astype(jnp.bfloat16)


def lane_index(shape):
    return lax.broadcasted_iota(jnp.int32, shape, len(shape) - 1)


def fill_weights(out_ref, bias_ref, bin_ref, flat_weight, weight_ref):
    bins, heads = bin_ref.shape[0], bias_ref.shape[0]
    hidden = out_ref.shape[0]
    flat_weight[...] = jnp.zeros_like(flat_weight)
    flat_weight[:bins, :] = bin_ref[...] - bin_ref[bins - 1 :, :]
    flat_weight[bins : bins + heads, :] = bias_ref[...]
    weight = flat_weight[...].T
    high = weight.astype(jnp.bfloat16)
    rest = weight - high.astype(jnp.float32)
    middle = rest.astype(jnp.bfloat16)
    low = (rest - middle.astype(jnp.float32)).astype(jnp.bfloat16)
    parts = dot(out_ref[...], jnp.concatenate([high, middle, low], axis=1))
    folded = parts[:, :LANES] + parts[:, LANES : 2 * LANES] + parts[:, 2 * LANES :]
    folded_high, folded_low = split(folded)
    weight_ref[:hidden, :LANES] = folded_high
    weight_ref[:hidden, LANES:] = folded_low
    weight_ref[hidden:, :LANES] = high
    weight_ref[hidden:, LANES:] = middle


def pair_heads(pair_ref, gain, in_ref, weight_ref, heads_ref):
    rows, cols, channels = pair_ref.shape
    hidden = in_ref.shape[1] // 2
    for start in range(0, rows, PAIR_STEP):
        tokens = pair_ref[start : start + PAIR_STEP].reshape(PAIR_STEP * cols, channels)
        inner = centered(tokens.astype(jnp.float32)) * gain
        both = dot(inner.astype(jnp.bfloat16), in_ref[...])
        gate = both[:, :hidden] * 0.5
        gated = (gate * (1.0 + jnp.tanh(gate)) * both[:, hidden:]).astype(jnp.bfloat16)
        twice = dot(gated, weight_ref[:hidden, :]) + dot(tokens, weight_ref[hidden:, :])
        at = slice(start * cols, (start + PAIR_STEP) * cols)
        heads_ref[at, :] = twice[:, :LANES] + twice[:, LANES:]


def fill_code(bins, rows, cols, heads_ref, code_ref):
    half = rows // 2
    lanes = lane_index((half * CODE_GROUP, LANES))
    for start in range(0, cols, CODE_GROUP):
        first, second = (
            jnp.concatenate(
                [
                    heads_ref[pl.ds(top * cols + col, half, stride=cols), :]
                    for col in range(start, start + CODE_GROUP)
                ],
                axis=0,
            )
            for top in (0, half)
        )
        packed = jnp.where(lanes < bins, first, pltpu.roll(second, bins, 1))
        top = jnp.max(jnp.abs(packed), axis=1, keepdims=True)
        power = jnp.ceil(jnp.log2(jnp.maximum(top, 1e-30)))
        code = jnp.where(
            lanes % bins == bins - 1, power, packed * (jnp.exp2(-power) * CODE_TOP)
        )
        code = jnp.round(code).astype(jnp.int32).astype(jnp.int16)
        code_ref[start : start + CODE_GROUP] = code.reshape(CODE_GROUP, half, LANES)


def first_kernel(
    pair_ref,
    gain_ref,
    in_ref,
    out_ref,
    bias_ref,
    bin_ref,
    heads_ref,
    code_ref,
    later_ref,
    gain_near,
    in_near,
    weight_ref,
    tile,
    out_near,
    bias_near,
    bin_near,
    flat_weight,
    sems,
):
    rows, cols, _ = tile.shape

    def bring(source, target, sem):
        copy = pltpu.make_async_copy(source, target, sem)
        copy.start()
        return copy

    small = [
        bring(source, target, sems.at[k])
        for k, (source, target) in enumerate(
            ((bias_ref, bias_near), (bin_ref, bin_near), (out_ref, out_near))
        )
    ]
    gain_copy = bring(gain_ref, gain_near, sems.at[3])
    tile_copy = bring(pair_ref.at[:, pl.ds(0, cols)], tile, sems.at[4])
    in_copy = bring(in_ref, in_near, sems.at[5])
    later = bring(pair_ref.at[:, pl.ds(cols, later_ref.shape[1])], later_ref, sems.at[6])
    for copy in small:
        copy.wait()
    fill_weights(out_near, bias_near, bin_near, flat_weight, weight_ref)
    gain_copy.wait()
    in_copy.wait()
    tile_copy.wait()
    gain = gain_near[...].reshape(1, -1)
    pair_heads(tile, gain, in_near, weight_ref, heads_ref)
    fill_code(bin_ref.shape[0], rows, cols, heads_ref, code_ref)
    later.wait()


def second_kernel(bins, pair_ref, gain_ref, in_ref, weight_ref, heads_ref, code_ref):
    rows, cols, _ = pair_ref.shape
    gain = gain_ref[...].reshape(1, -1)
    pair_heads(pair_ref, gain, in_ref, weight_ref, heads_ref)
    fill_code(bins, rows, cols, heads_ref, code_ref)


def apart(size):
    return size // 2


def softmax_kernel(part, turn, most, size, heads, first_ref, second_ref, code_ref, *refs):
    if turn == 2:
        parts, (gates_ref, weight_ref, _) = refs[:size], refs[size : size + 3]
        out_ref, single_ref, held, sems, single_held, single_sem = refs[size + 3 :]
    else:
        out_ref, held, sems = refs[-3:]
    rows, cols, bins = held.shape
    half = cols // 2
    distance = lax.axis_index("col") - lax.axis_index("row")
    relayed = (distance == apart(size)) | (distance == apart(size) - size)
    begin = first_ref.shape[1] if part else 0

    def own(side, at):
        cut = first_ref.shape[1]
        low, high = side * half, (side + 1) * half
        pieces = []
        if low < cut:
            pieces.append(first_ref[at, low : min(high, cut)])
        if high > cut:
            pieces.append(second_ref[at, max(low - cut, 0) : high - cut])
        return jnp.concatenate(pieces, axis=1).reshape(-1, LANES)

    def work():
        copies = []
        for start in range(0, rows, most):
            step = min(most, rows - start)
            lanes = lane_index((step * half, LANES))
            low = lanes < bins
            code = code_ref[start : start + step]
            if turn == 0:
                code = lax.select_n(distance == 0, code, refs[0][start : start + step])
            code = code.reshape(step * half, LANES)
            code = code.astype(jnp.int32).astype(jnp.float32)
            power = jnp.sum(jnp.where(lanes == bins - 1, code, 0.0), axis=1, keepdims=True)
            other = code * (jnp.exp2(power) * (1.0 / CODE_TOP))
            other = jnp.where(lanes % bins == bins - 1, 0.0, other)
            at = slice(begin + start, begin + start + step)
            for side in range(2):
                mirrored = other if side == 0 else pltpu.roll(other, bins, 1)
                logits = jnp.where(low, own(side, at) + mirrored, -jnp.inf)
                top = jnp.max(logits, axis=1, keepdims=True)
                raised = jnp.exp(logits - top)
                share = raised * (1.0 / jnp.sum(raised, axis=1, keepdims=True))
                held[start : start + step, side * half : (side + 1) * half, :] = share[
                    :, :bins
                ].reshape(step, half, bins)
            copies.append(
                pltpu.make_async_copy(
                    held.at[pl.ds(start, step)],
                    out_ref.at[pl.ds(begin + start, step)],
                    sems.at[start // most],
                )
            )
            copies[-1].start()
        for copy in copies:
            copy.wait()

    if turn == 2:
        single_held[...] = joined(heads, parts, gates_ref, weight_ref)
        single_copy = pltpu.make_async_copy(single_held, single_ref, single_sem)
        single_copy.start()
    if turn == 1:
        work()
    else:
        pl.when(relayed if turn == 2 else jnp.logical_not(relayed))(work)
    if turn == 2:
        single_copy.wait()


def attention_kernel(
    bins,
    single_ref,
    keys_ref,
    mask_ref,
    gain_ref,
    in_ref,
    first_ref,
    second_ref,
    part_ref,
    gates_ref,
    scores,
):
    rows, width = single_ref.shape
    heads, cols = scores.shape[1:]
    head_width = width // heads
    gain = gain_ref[...].reshape(1, -1)
    query_inner = (centered(single_ref[...].astype(jnp.float32)) * gain).astype(jnp.bfloat16)
    key_inner = (centered(keys_ref[...].astype(jnp.float32)) * gain).astype(jnp.bfloat16)
    queries = dot(query_inner, in_ref[:, :width]) * (1.0 / math.sqrt(head_width))
    gates_ref[...] = jax.nn.sigmoid(dot(query_inner, in_ref[:, 3 * width :]))
    keys_proj = dot(key_inner, in_ref[:, width : 2 * width]).astype(jnp.bfloat16)
    values_proj = dot(key_inner, in_ref[:, 2 * width : 3 * width]).astype(jnp.bfloat16)
    shape = (heads, width)
    lane = lane_index(shape)
    head = lax.broadcasted_iota(jnp.int32, shape, 0)
    own_head = jnp.where((lane >= head * head_width) & (lane < (head + 1) * head_width), 1.0, 0.0)
    spread = (queries[:, None, :] * own_head[None]).astype(jnp.bfloat16)
    scores[...] = dot_t(spread.reshape(rows * heads, width), keys_proj).reshape(rows, heads, cols)
    shape = (heads, 2 * LANES)
    lane = lane_index(shape) % LANES
    pick = (lane == lax.broadcasted_iota(jnp.int32, shape, 0) + bins).astype(jnp.bfloat16)
    for row in range(rows):
        block = jnp.concatenate(
            [first_ref[row], second_ref[row]], axis=0
        )
        scores[row] += dot_t(pick, jnp.concatenate(split(block), axis=1))
    kept = jnp.where(mask_ref[...].reshape(1, -1) > 0, scores[...].reshape(rows * heads, cols), -1000000000.0)
    top = jnp.max(kept, axis=-1, keepdims=True)
    weights = jnp.exp(kept - top)
    total = jnp.sum(weights, axis=-1, keepdims=True)
    summed = dot((weights * (1.0 / total)).astype(jnp.bfloat16), values_proj)
    summed = jnp.sum(summed.reshape(rows, heads, width) * own_head[None], axis=1)
    part_ref[:, :width] = summed.astype(jnp.bfloat16)
    level = top + jnp.log(total)
    high = level.astype(jnp.bfloat16).astype(jnp.float32)
    middle = (level - high).astype(jnp.bfloat16).astype(jnp.float32)
    low = level - high - middle
    shape = (heads, LANES)
    lane = lane_index(shape)
    head = lax.broadcasted_iota(jnp.int32, shape, 0)
    spread = jnp.zeros((rows, heads, LANES), jnp.float32)
    for place, piece in enumerate((high, middle, low)):
        at = (lane == head + place * heads).astype(jnp.float32)
        spread += piece.reshape(rows, heads, 1) * at[None]
    part_ref[:, width:] = jnp.sum(spread, axis=1).astype(jnp.bfloat16)


def joined(heads, parts, gates_ref, out_weight_ref):
    width = gates_ref.shape[1]
    head_width = width // heads
    shape = (LANES, width)
    lane = lane_index(shape)
    row = lax.broadcasted_iota(jnp.int32, shape, 0)
    head = row % heads
    spread = (
        (lane >= head * head_width) & (lane < (head + 1) * head_width) & (row < 3 * heads)
    ).astype(jnp.bfloat16)
    levels = [dot(part[:, width:], spread) for part in parts]
    top = functools.reduce(jnp.maximum, levels)
    total, summed = 0.0, 0.0
    for level, part in zip(levels, parts):
        factor = jnp.exp(level - top)
        total += factor
        summed += factor * part[:, :width].astype(jnp.float32)
    gated = (gates_ref[...] * (summed / total)).astype(jnp.bfloat16)
    return dot(gated, out_weight_ref[...]).astype(jnp.bfloat16)


def partner(place, away, size):
    return place ^ away if size & (size - 1) == 0 else (place + away) % size


def body(
    row_count,
    col_count,
    pair,
    single,
    token_mask,
    pair_gain,
    transition_in,
    transition_out,
    bias_weight,
    bin_weight,
    single_gain,
    attention_in,
    attention_out,
):
    rows, cols, channels = pair.shape
    width = single.shape[1]
    heads, bins = bias_weight.shape[1], bin_weight.shape[1]
    hidden = transition_out.shape[0]
    cut = cols * 5 // 8 // ROW_TILE * ROW_TILE
    rest = cols - cut
    grid = [(r, c) for r in range(row_count) for c in range(col_count)]
    far = [(r, c) for r, c in grid if c == (r + apart(col_count)) % col_count]

    def moved(value, pairs):
        pairs = [(a * col_count + b, c * col_count + d) for (a, b), (c, d) in pairs]
        return lax.ppermute(value, ("row", "col"), pairs)

    mirror = [((r, c), (c, r)) for r, c in grid]
    near_mirror = [((r, c), (c, r)) for r, c in grid if r != c and (r, c) not in far]
    to_relay = [((r, c), (r, r)) for r, c in far]
    from_relay = [((r, r), (c, r)) for r, c in far]
    half_way = [((c, (r + apart(col_count)) % col_count), (r, c)) for r, c in grid]
    bf16, f32, i16 = jnp.bfloat16, jnp.float32, jnp.int16
    first, code, later, *kept = call(
        first_kernel,
        (
            near((rows * cut, LANES), f32),
            near((cut, rows // 2, LANES), i16),
            near((rows, rest, channels), bf16),
            near(pair_gain.shape, f32),
            near(transition_in.shape, bf16),
            near((hidden + channels, 2 * LANES), bf16),
        ),
        (pair, pair_gain, transition_in, transition_out, bias_weight.T, bin_weight.T),
        scratch=(
            pltpu.VMEM((rows, cut, channels), bf16),
            pltpu.VMEM(transition_out.shape, bf16),
            pltpu.VMEM((heads, channels), f32),
            pltpu.VMEM((bins, channels), f32),
            pltpu.VMEM((LANES, channels), f32),
            pltpu.SemaphoreType.DMA((7,)),
        ),
        far=range(6),
    )
    own_code, early = code, moved(code, near_mirror + to_relay)
    behind, _ = lax.optimization_barrier((single, code))
    keys = moved(behind, half_way)
    second, code = call(
        functools.partial(second_kernel, bins),
        (near((rows * rest, LANES), f32), near((rest, rows // 2, LANES), i16)),
        (later, *kept),
    )
    own = (first.reshape(rows, cut, LANES), second.reshape(rows, rest, LANES))
    code, keys = lax.optimization_barrier((code, keys))
    direct = moved(code, mirror)
    passed, _ = lax.optimization_barrier((early, code))
    relayed = moved(passed, from_relay)
    part_sums, gates = call(
        functools.partial(attention_kernel, bins),
        (
            near((rows, width + LANES), jnp.bfloat16),
            near((rows, width), jnp.float32),
        ),
        (single, keys, token_mask, single_gain, attention_in, *own),
        scratch=(pltpu.VMEM((rows, heads, cols), jnp.float32),),
    )
    parts = [part_sums]
    for away in [*range(2, col_count), 1]:
        ring = [(c, partner(c, away, col_count)) for c in range(col_count)]
        parts.append(lax.ppermute(part_sums, "col", ring))
    distogram_out = jax.ShapeDtypeStruct((rows, cols, bins), f32)
    single_out = jax.ShapeDtypeStruct((rows, width), bf16)

    def turn(number, part, codes, outs, more=(), scratch=()):
        count = codes[0].shape[0]
        blocks = -(-count // SOFT_STEP)
        scratch = (
            pltpu.VMEM((count, cols, bins), f32),
            pltpu.SemaphoreType.DMA((blocks,)),
            *scratch,
        )
        last = 2 + len(codes) + len(more) - 1
        return call(
            functools.partial(softmax_kernel, part, number, SOFT_STEP, col_count, heads),
            outs,
            (*own, *codes, *more),
            scratch=scratch,
            far=(last,) if number else (),
            aliases={last: 0} if number else {},
        )

    distogram = turn(0, 0, (early, own_code), distogram_out)
    distogram = turn(1, 1, (direct,), distogram_out, (distogram,))
    distogram, single_update = turn(
        2,
        0,
        (relayed,),
        (distogram_out, single_out),
        (*parts, gates, attention_out, distogram),
        scratch=(pltpu.VMEM((rows, width), bf16), pltpu.SemaphoreType.DMA),
    )
    return (distogram, single_update)


def solution(mesh):
    in_specs = (
        P(("groups", "row"), "col", None),
        P(("groups", "row"), None),
        P(("groups", "col")),
        P(),
        P(),
        P(),
        P(),
        P(),
        P(),
        P(),
        P(),
    )
    out_specs = (P(("groups", "row"), "col", None), P(("groups", "row"), None))
    own = functools.partial(body, mesh.shape["row"], mesh.shape["col"])
    return jax.shard_map(own, mesh=mesh, in_specs=in_specs, out_specs=out_specs, check_vma=False)
```

```python
import functools
import math

import jax
import jax.numpy as jnp
from jax import lax
from jax.experimental import pallas as pl
from jax.experimental.pallas import tpu as pltpu
from jax.sharding import PartitionSpec as P

LANES = 128
CODE_TOP = 32767.0
PAIR_STEP = 8
CODE_GROUP = 8
SOFT_STEP = 16
ROW_TILE = 8
VMEM_LIMIT = 56 * 1024 * 1024


def near(shape, dtype):
    return pltpu.VMEM(shape, dtype)


def call(kernel, outs, args, scratch=(), far=(), aliases=None):
    def out_spec(out):
        inside = isinstance(out, type(near((8, LANES), jnp.float32)))
        return pl.BlockSpec(memory_space=pltpu.VMEM if inside else pl.ANY)

    return pl.pallas_call(
        kernel,
        out_shape=outs,
        in_specs=[
            pl.BlockSpec(memory_space=pl.ANY if k in far else pltpu.VMEM) for k in range(len(args))
        ],
        out_specs=jax.tree.map(out_spec, outs),
        scratch_shapes=list(scratch),
        input_output_aliases=aliases or {},
        compiler_params=pltpu.CompilerParams(vmem_limit_bytes=VMEM_LIMIT),
    )(
        *[
            a if k in far else pltpu.with_memory_space_constraint(a, pltpu.VMEM)
            for k, a in enumerate(args)
        ]
    )


def centered(values):
    rest = values - jnp.mean(values, axis=-1, keepdims=True)
    variance = jnp.mean(rest * rest, axis=-1, keepdims=True)
    return rest * lax.rsqrt(variance + 1e-05)


def dot(a, b):
    return jnp.dot(a, b, preferred_element_type=jnp.float32)


def dot_t(a, b):
    return lax.dot_general(a, b, (((1,), (1,)), ((), ())), preferred_element_type=jnp.float32)


def split(value):
    high = value.astype(jnp.bfloat16)
    return high, (value - high.astype(jnp.float32)).astype(jnp.bfloat16)


def lane_index(shape):
    return lax.broadcasted_iota(jnp.int32, shape, len(shape) - 1)


def fill_weights(out_ref, bias_ref, bin_ref, flat_weight, weight_ref):
    bins, heads = bin_ref.shape[0], bias_ref.shape[0]
    hidden = out_ref.shape[0]
    flat_weight[...] = jnp.zeros_like(flat_weight)
    flat_weight[:bins, :] = bin_ref[...] - bin_ref[bins - 1 :, :]
    flat_weight[bins : bins + heads, :] = bias_ref[...]
    weight = flat_weight[...].T
    high = weight.astype(jnp.bfloat16)
    rest = weight - high.astype(jnp.float32)
    middle = rest.astype(jnp.bfloat16)
    low = (rest - middle.astype(jnp.float32)).astype(jnp.bfloat16)
    parts = dot(out_ref[...], jnp.concatenate([high, middle, low], axis=1))
    folded = parts[:, :LANES] + parts[:, LANES : 2 * LANES] + parts[:, 2 * LANES :]
    folded_high, folded_low = split(folded)
    weight_ref[:hidden, :LANES] = folded_high
    weight_ref[:hidden, LANES:] = folded_low
    weight_ref[hidden:, :LANES] = high
    weight_ref[hidden:, LANES:] = middle


def pair_heads(pair_ref, gain, in_ref, weight_ref, heads_ref):
    rows, cols, channels = pair_ref.shape
    hidden = in_ref.shape[1] // 2
    for start in range(0, rows, PAIR_STEP):
        tokens = pair_ref[start : start + PAIR_STEP].reshape(PAIR_STEP * cols, channels)
        inner = centered(tokens.astype(jnp.float32)) * gain
        both = dot(inner.astype(jnp.bfloat16), in_ref[...])
        gate = both[:, :hidden] * 0.5
        gated = (gate * (1.0 + jnp.tanh(gate)) * both[:, hidden:]).astype(jnp.bfloat16)
        twice = dot(gated, weight_ref[:hidden, :]) + dot(tokens, weight_ref[hidden:, :])
        at = slice(start * cols, (start + PAIR_STEP) * cols)
        heads_ref[at, :] = twice[:, :LANES] + twice[:, LANES:]


def fill_code(bins, rows, cols, heads_ref, code_ref):
    half = rows // 2
    lanes = lane_index((half * CODE_GROUP, LANES))
    for start in range(0, cols, CODE_GROUP):
        first, second = (
            jnp.concatenate(
                [
                    heads_ref[pl.ds(top * cols + col, half, stride=cols), :]
                    for col in range(start, start + CODE_GROUP)
                ],
                axis=0,
            )
            for top in (0, half)
        )
        packed = jnp.where(lanes < bins, first, pltpu.roll(second, bins, 1))
        top = jnp.max(jnp.abs(packed), axis=1, keepdims=True)
        power = jnp.ceil(jnp.log2(jnp.maximum(top, 1e-30)))
        code = jnp.where(
            lanes % bins == bins - 1, power, packed * (jnp.exp2(-power) * CODE_TOP)
        )
        code = jnp.round(code).astype(jnp.int32).astype(jnp.int16)
        code_ref[start : start + CODE_GROUP] = code.reshape(CODE_GROUP, half, LANES)


def first_kernel(
    pair_ref,
    gain_ref,
    in_ref,
    out_ref,
    bias_ref,
    bin_ref,
    heads_ref,
    code_ref,
    later_ref,
    gain_near,
    in_near,
    weight_ref,
    tile,
    out_near,
    bias_near,
    bin_near,
    flat_weight,
    sems,
):
    rows, cols, _ = tile.shape

    def bring(source, target, sem):
        copy = pltpu.make_async_copy(source, target, sem)
        copy.start()
        return copy

    small = [
        bring(source, target, sems.at[k])
        for k, (source, target) in enumerate(
            ((bias_ref, bias_near), (bin_ref, bin_near), (out_ref, out_near))
        )
    ]
    gain_copy = bring(gain_ref, gain_near, sems.at[3])
    tile_copy = bring(pair_ref.at[:, pl.ds(0, cols)], tile, sems.at[4])
    in_copy = bring(in_ref, in_near, sems.at[5])
    later = bring(pair_ref.at[:, pl.ds(cols, later_ref.shape[1])], later_ref, sems.at[6])
    for copy in small:
        copy.wait()
    fill_weights(out_near, bias_near, bin_near, flat_weight, weight_ref)
    gain_copy.wait()
    in_copy.wait()
    tile_copy.wait()
    gain = gain_near[...].reshape(1, -1)
    pair_heads(tile, gain, in_near, weight_ref, heads_ref)
    fill_code(bin_ref.shape[0], rows, cols, heads_ref, code_ref)
    later.wait()


def second_kernel(bins, pair_ref, gain_ref, in_ref, weight_ref, heads_ref, code_ref):
    rows, cols, _ = pair_ref.shape
    gain = gain_ref[...].reshape(1, -1)
    pair_heads(pair_ref, gain, in_ref, weight_ref, heads_ref)
    fill_code(bins, rows, cols, heads_ref, code_ref)


def apart(size):
    return size // 2


def softmax_kernel(part, turn, most, size, first_ref, second_ref, code_ref, *refs):
    out_ref, held, sems = refs[-3:]
    rows, cols, bins = held.shape
    half = cols // 2
    distance = lax.axis_index("col") - lax.axis_index("row")
    relayed = (distance == apart(size)) | (distance == apart(size) - size)
    begin = first_ref.shape[1] if part else 0

    def own(side, at):
        cut = first_ref.shape[1]
        low, high = side * half, (side + 1) * half
        pieces = []
        if low < cut:
            pieces.append(first_ref[at, low : min(high, cut)])
        if high > cut:
            pieces.append(second_ref[at, max(low - cut, 0) : high - cut])
        return jnp.concatenate(pieces, axis=1).reshape(-1, LANES)

    def work():
        copies = []
        for start in range(0, rows, most):
            step = min(most, rows - start)
            lanes = lane_index((step * half, LANES))
            low = lanes < bins
            code = code_ref[start : start + step]
            if turn == 0:
                code = lax.select_n(distance == 0, code, refs[0][start : start + step])
            code = code.reshape(step * half, LANES)
            code = code.astype(jnp.int32).astype(jnp.float32)
            power = jnp.sum(jnp.where(lanes == bins - 1, code, 0.0), axis=1, keepdims=True)
            other = code * (jnp.exp2(power) * (1.0 / CODE_TOP))
            other = jnp.where(lanes % bins == bins - 1, 0.0, other)
            at = slice(begin + start, begin + start + step)
            for side in range(2):
                mirrored = other if side == 0 else pltpu.roll(other, bins, 1)
                logits = jnp.where(low, own(side, at) + mirrored, -jnp.inf)
                top = jnp.max(logits, axis=1, keepdims=True)
                raised = jnp.exp(logits - top)
                share = raised * (1.0 / jnp.sum(raised, axis=1, keepdims=True))
                held[start : start + step, side * half : (side + 1) * half, :] = share[
                    :, :bins
                ].reshape(step, half, bins)
            copies.append(
                pltpu.make_async_copy(
                    held.at[pl.ds(start, step)],
                    out_ref.at[pl.ds(begin + start, step)],
                    sems.at[start // most],
                )
            )
            copies[-1].start()
        for copy in copies:
            copy.wait()

    if turn == 1:
        work()
    else:
        pl.when(relayed if turn == 2 else jnp.logical_not(relayed))(work)


def attention_kernel(
    bins,
    single_ref,
    keys_ref,
    mask_ref,
    gain_ref,
    in_ref,
    first_ref,
    second_ref,
    part_ref,
    gates_ref,
    scores,
):
    rows, width = single_ref.shape
    heads, cols = scores.shape[1:]
    head_width = width // heads
    gain = gain_ref[...].reshape(1, -1)
    query_inner = (centered(single_ref[...].astype(jnp.float32)) * gain).astype(jnp.bfloat16)
    key_inner = (centered(keys_ref[...].astype(jnp.float32)) * gain).astype(jnp.bfloat16)
    queries = dot(query_inner, in_ref[:, :width]) * (1.0 / math.sqrt(head_width))
    gates_ref[...] = jax.nn.sigmoid(dot(query_inner, in_ref[:, 3 * width :]))
    keys_proj = dot(key_inner, in_ref[:, width : 2 * width]).astype(jnp.bfloat16)
    values_proj = dot(key_inner, in_ref[:, 2 * width : 3 * width]).astype(jnp.bfloat16)
    shape = (heads, width)
    lane = lane_index(shape)
    head = lax.broadcasted_iota(jnp.int32, shape, 0)
    own_head = jnp.where((lane >= head * head_width) & (lane < (head + 1) * head_width), 1.0, 0.0)
    spread = (queries[:, None, :] * own_head[None]).astype(jnp.bfloat16)
    scores[...] = dot_t(spread.reshape(rows * heads, width), keys_proj).reshape(rows, heads, cols)
    shape = (heads, 2 * LANES)
    lane = lane_index(shape) % LANES
    pick = (lane == lax.broadcasted_iota(jnp.int32, shape, 0) + bins).astype(jnp.bfloat16)
    for row in range(rows):
        block = jnp.concatenate(
            [first_ref[row], second_ref[row]], axis=0
        )
        scores[row] += dot_t(pick, jnp.concatenate(split(block), axis=1))
    kept = jnp.where(mask_ref[...].reshape(1, -1) > 0, scores[...].reshape(rows * heads, cols), -1000000000.0)
    top = jnp.max(kept, axis=-1, keepdims=True)
    weights = jnp.exp(kept - top)
    total = jnp.sum(weights, axis=-1, keepdims=True)
    summed = dot((weights * (1.0 / total)).astype(jnp.bfloat16), values_proj)
    summed = jnp.sum(summed.reshape(rows, heads, width) * own_head[None], axis=1)
    part_ref[:, :width] = summed.astype(jnp.bfloat16)
    level = top + jnp.log(total)
    high = level.astype(jnp.bfloat16).astype(jnp.float32)
    middle = (level - high).astype(jnp.bfloat16).astype(jnp.float32)
    low = level - high - middle
    shape = (heads, LANES)
    lane = lane_index(shape)
    head = lax.broadcasted_iota(jnp.int32, shape, 0)
    spread = jnp.zeros((rows, heads, LANES), jnp.float32)
    for place, piece in enumerate((high, middle, low)):
        at = (lane == head + place * heads).astype(jnp.float32)
        spread += piece.reshape(rows, heads, 1) * at[None]
    part_ref[:, width:] = jnp.sum(spread, axis=1).astype(jnp.bfloat16)


def joined(heads, parts, gates_ref, out_weight_ref):
    width = gates_ref.shape[1]
    head_width = width // heads
    shape = (LANES, width)
    lane = lane_index(shape)
    row = lax.broadcasted_iota(jnp.int32, shape, 0)
    head = row % heads
    spread = (
        (lane >= head * head_width) & (lane < (head + 1) * head_width) & (row < 3 * heads)
    ).astype(jnp.bfloat16)
    levels = [dot(part[:, width:], spread) for part in parts]
    top = functools.reduce(jnp.maximum, levels)
    total, summed = 0.0, 0.0
    for level, part in zip(levels, parts):
        factor = jnp.exp(level - top)
        total += factor
        summed += factor * part[:, :width].astype(jnp.float32)
    gated = (gates_ref[...] * (summed / total)).astype(jnp.bfloat16)
    return dot(gated, out_weight_ref[...]).astype(jnp.bfloat16)


def joined_kernel(heads, count, *refs):
    parts, (gates_ref, weight_ref, out_ref, held, sem) = refs[:count], refs[count:]
    held[...] = joined(heads, parts, gates_ref, weight_ref)
    copy = pltpu.make_async_copy(held, out_ref, sem)
    copy.start()
    copy.wait()


def partner(place, away, size):
    return place ^ away if size & (size - 1) == 0 else (place + away) % size


def body(
    row_count,
    col_count,
    pair,
    single,
    token_mask,
    pair_gain,
    transition_in,
    transition_out,
    bias_weight,
    bin_weight,
    single_gain,
    attention_in,
    attention_out,
):
    rows, cols, channels = pair.shape
    width = single.shape[1]
    heads, bins = bias_weight.shape[1], bin_weight.shape[1]
    hidden = transition_out.shape[0]
    cut = cols * 5 // 8 // ROW_TILE * ROW_TILE
    rest = cols - cut
    grid = [(r, c) for r in range(row_count) for c in range(col_count)]
    far = [(r, c) for r, c in grid if c == (r + apart(col_count)) % col_count]

    def moved(value, pairs):
        pairs = [(a * col_count + b, c * col_count + d) for (a, b), (c, d) in pairs]
        return lax.ppermute(value, ("row", "col"), pairs)

    mirror = [((r, c), (c, r)) for r, c in grid]
    near_mirror = [((r, c), (c, r)) for r, c in grid if r != c and (r, c) not in far]
    to_relay = [((r, c), (r, r)) for r, c in far]
    from_relay = [((r, r), (c, r)) for r, c in far]
    half_way = [((c, (r + apart(col_count)) % col_count), (r, c)) for r, c in grid]
    bf16, f32, i16 = jnp.bfloat16, jnp.float32, jnp.int16
    first, code, later, *kept = call(
        first_kernel,
        (
            near((rows * cut, LANES), f32),
            near((cut, rows // 2, LANES), i16),
            near((rows, rest, channels), bf16),
            near(pair_gain.shape, f32),
            near(transition_in.shape, bf16),
            near((hidden + channels, 2 * LANES), bf16),
        ),
        (pair, pair_gain, transition_in, transition_out, bias_weight.T, bin_weight.T),
        scratch=(
            pltpu.VMEM((rows, cut, channels), bf16),
            pltpu.VMEM(transition_out.shape, bf16),
            pltpu.VMEM((heads, channels), f32),
            pltpu.VMEM((bins, channels), f32),
            pltpu.VMEM((LANES, channels), f32),
            pltpu.SemaphoreType.DMA((7,)),
        ),
        far=range(6),
    )
    own_code, early = code, moved(code, near_mirror + to_relay)
    behind, _ = lax.optimization_barrier((single, code))
    keys = moved(behind, half_way)
    second, code = call(
        functools.partial(second_kernel, bins),
        (near((rows * rest, LANES), f32), near((rest, rows // 2, LANES), i16)),
        (later, *kept),
    )
    own = (first.reshape(rows, cut, LANES), second.reshape(rows, rest, LANES))
    code, keys = lax.optimization_barrier((code, keys))
    direct = moved(code, mirror)
    passed, _ = lax.optimization_barrier((early, code))
    relayed = moved(passed, from_relay)
    part_sums, gates = call(
        functools.partial(attention_kernel, bins),
        (
            near((rows, width + LANES), jnp.bfloat16),
            near((rows, width), jnp.float32),
        ),
        (single, keys, token_mask, single_gain, attention_in, *own),
        scratch=(pltpu.VMEM((rows, heads, cols), jnp.float32),),
    )
    parts = [part_sums]
    for away in [*range(2, col_count), 1]:
        ring = [(c, partner(c, away, col_count)) for c in range(col_count)]
        parts.append(lax.ppermute(part_sums, "col", ring))
    distogram_out = jax.ShapeDtypeStruct((rows, cols, bins), f32)
    single_out = jax.ShapeDtypeStruct((rows, width), bf16)

    def turn(number, part, codes, outs, more=()):
        count = codes[0].shape[0]
        blocks = -(-count // SOFT_STEP)
        scratch = (pltpu.VMEM((count, cols, bins), f32), pltpu.SemaphoreType.DMA((blocks,)))
        last = 2 + len(codes) + len(more) - 1
        return call(
            functools.partial(softmax_kernel, part, number, SOFT_STEP, col_count),
            outs,
            (*own, *codes, *more),
            scratch=scratch,
            far=(last,) if number else (),
            aliases={last: 0} if number else {},
        )

    distogram = turn(0, 0, (early, own_code), distogram_out)
    distogram = turn(1, 1, (direct,), distogram_out, (distogram,))
    distogram = turn(2, 0, (relayed,), distogram_out, (distogram,))
    *parts, distogram = lax.optimization_barrier((*parts, distogram))
    single_update = call(
        functools.partial(joined_kernel, heads, col_count),
        single_out,
        (*parts, gates, attention_out),
        scratch=(pltpu.VMEM((rows, width), bf16), pltpu.SemaphoreType.DMA),
    )
    return (distogram, single_update)


def solution(mesh):
    in_specs = (
        P(("groups", "row"), "col", None),
        P(("groups", "row"), None),
        P(("groups", "col")),
        P(),
        P(),
        P(),
        P(),
        P(),
        P(),
        P(),
        P(),
    )
    out_specs = (P(("groups", "row"), "col", None), P(("groups", "row"), None))
    own = functools.partial(body, mesh.shape["row"], mesh.shape["col"])
    return jax.shard_map(own, mesh=mesh, in_specs=in_specs, out_specs=out_specs, check_vma=False)
```
